128 devices in a mesh: dp: 16 (over x, z_hi, core), ctx: 8 (over y, z_lo).
Axes of the slice: x: 4, y: 4, z: 4 (z_hi: 2, z_lo: 2; z = z_hi * 2 + z_lo), core: 2. Of those that a mesh axis runs over, the one named last changes fastest.
Arguments:
- inputs: bfloat16 [16, 2, 8, 128, 2048], P('dp', None, 'ctx'), may hold values from -6 to 6
- norm_gain_vector: float32 [2048], replicated, may hold values from 0.1 to 1.9
- w_qkv: bfloat16 [2048, 3072], replicated, may hold values from -2.6958446 to 2.6958446
- doc_lengths: int32 [16, 16], P('dp'), may hold values from 1 to 1024, 2048 in all within a row
- out_grad: bfloat16 [16, 2, 8, 128, 2048], P('dp', None, 'ctx'), may hold values from -6 to 6
Outputs:
- attended: bfloat16 [16, 2, 8, 128, 2048], P('dp', None, 'ctx')
- inputs_grad: bfloat16 [16, 2, 8, 128, 2048], P('dp', None, 'ctx')
- qkv_grad: float32 [2048, 3072], P(('dp', 'ctx'))
- gain_grad: float32 [2048], P(('dp', 'ctx'))
The draws below stay inside these ranges and needn't reach their ends.
Inputs may be any that keep to these rules, and one draw needn't show every extreme that they name: `doc_lengths`: each row holds the lengths of the documents of one episode, which sum to 2048.
All inputs are finite; a program needn't handle non-finite values.
Results may differ from the reference program's by a relative error of at most 0.012.
Values may be sent and summed in bfloat16 or wider, within the bound.
No kernel may reach another device: no remote copies, remote signals or barrier semaphores. Data moves between devices by JAX's collectives and lax.ppermute only.
A program may use at most 128 MiB of HBM per device.

```python
import math
import jax
import jax.numpy as jnp
import numpy as np
from jax import lax

D = 2048
HEAD = 128
KVH = 4
GROUP = 4
DOCS = 16
HALF = 128
SEQ = 2048
EPIS = 16
QCOLS = 2048
N_CTX = 8


def draw_w_qkv(key, part):
    width_all = KVH * (GROUP + 2) * HEAD
    normal_draw = jax.random.truncated_normal(key, -6.0, 6.0, (D, width_all), jnp.float32) * D ** (-0.5)
    return normal_draw.astype(jnp.bfloat16)


def block_scale(key, shape, pieces, least, high):
    gain, own = 1.0, jax.random.fold_in(key, 6)
    for position, shards_of in pieces:
        steps = jnp.exp(jax.random.uniform(jax.random.fold_in(own, position), (shards_of,), jnp.float32, least / len(pieces), high / len(pieces)))
        gain = gain * jnp.repeat(steps, shape[position] // shards_of).reshape([-1 if axis == position else 1 for axis in range(len(shape))])
    return gain


def length_profile(number_of, total, bound, skew):
    portions = [(1 << 20) // math.isqrt(grade ** skew) + 1 for grade in range(2, number_of + 1)]
    spare, counts = total - bound - (number_of - 1), [1] * (number_of - 1)
    while spare > 0:
        movable = [i for i in range(number_of - 1) if counts[i] < bound]
        mass, budget = sum([portions[i] for i in movable]), spare
        for i in movable:
            addition = min(bound - counts[i], max(1, budget * portions[i] // mass), spare)
            counts[i] = counts[i] + addition
            spare = spare - addition
    return np.array([bound] + counts)


def uneven(stream_key, number_of, total, most, skew):
    if number_of == 2:
        one = jax.random.randint(stream_key, (), max(1, total - most), min(most, total - 1) + 1)
        return jnp.stack([one, total - one])
    tallies = jnp.asarray(length_profile(number_of, total, most, skew), jnp.int32)
    couples = (number_of - 1) // 2
    giver, receiver = tallies[1:1 + 2 * couples:2], tallies[2:2 + 2 * couples:2]
    room = jnp.minimum(giver - 1, most - receiver)
    shifted = jax.random.randint(jax.random.fold_in(stream_key, 1), (couples,), 0, 1 << 20) % (room + 1)
    tallies = tallies.at[1:1 + 2 * couples:2].set(giver - shifted).at[2:2 + 2 * couples:2].set(receiver + shifted)
    return tallies[jax.random.permutation(jax.random.fold_in(stream_key, 2), number_of)]


def centred(rng, extent, deviation, limit, cuts=(), held_as=jnp.bfloat16):
    entries = jax.random.normal(rng, extent, jnp.float32) * deviation
    if len(cuts) > 0:
        entries = block_scale(rng, extent, cuts, -0.22, 0.18) * entries
    return jnp.clip(entries, min=-limit, max=limit).astype(held_as)


def setup_inputs(seed: int = 0) -> dict:
    splits = jax.random.split(jax.random.key(seed), 6)
    return {
        "inputs": centred(splits[0], (EPIS, 2, N_CTX, HALF, D), 1.0, 6.0, ((0, 16), (2, 8))),
        "norm_gain_vector": jnp.clip(1.0 + 0.18 * jax.random.normal(splits[1], (D,), jnp.float32), 0.1, 1.9),
        "w_qkv": draw_w_qkv(jax.random.fold_in(splits[5], 71), 0),
        "doc_lengths": jax.vmap(lambda own: uneven(own, DOCS, SEQ, SEQ // 2, 2))(jax.random.split(splits[3], EPIS)).reshape((EPIS, DOCS)).astype(jnp.int32),
        "out_grad": centred(splits[4], (EPIS, 2, N_CTX, HALF, QCOLS), 1.0, 6.0, ((0, 16), (2, 8))),
    }


norm_eps = 1e-05
rope_base = 500000.0

def rope_tables(positions, head_width):
    freq_index = jnp.arange(head_width // 2, dtype=jnp.float32)
    frequency = jnp.power(jnp.float32(rope_base), -2.0 * freq_index / head_width)
    angles = positions.astype(jnp.float32)[:, None] * frequency[None, :]
    return (jnp.cos(angles), jnp.sin(angles))

def rotate_pairs(vectors, cos_table, sin_table):
    half_len = vectors.shape[-1] // 2
    first_half = vectors[..., :half_len]
    second = vectors[..., half_len:]
    return jnp.concatenate([first_half * cos_table - second * sin_table, second * cos_table + first_half * sin_table], axis=-1)

def layout_positions(ctx_size, half_len):
    which_half = jnp.arange(2, dtype=jnp.int32)[:, None, None]
    blocks = jnp.arange(ctx_size, dtype=jnp.int32)[None, :, None]
    offset = jnp.arange(half_len, dtype=jnp.int32)[None, None, :]
    return jnp.where(which_half == 0, blocks * half_len + offset, (2 * ctx_size - 1 - blocks) * half_len + offset).reshape(-1)

def document_ids(positions, lengths):
    doc_ends = jnp.cumsum(lengths).astype(jnp.int32)
    return lax.optimization_barrier(jnp.sum((positions[:, None] >= doc_ends[None, :]).astype(jnp.int32), axis=1))

def episode(inputs, lengths, out_grad, norm_gain_vector, w_qkv):
    local_count = 2 * N_CTX * HALF
    query_cols = KVH * GROUP * HEAD
    token_rows = inputs.reshape(local_count, D).astype(jnp.float32)
    positions = layout_positions(N_CTX, HALF)
    doc_ids = document_ids(positions, lengths)
    inverse_root = lax.rsqrt(lax.optimization_barrier(jnp.mean(token_rows * token_rows, axis=1, keepdims=True)) + norm_eps)
    unit_tokens = token_rows * inverse_root
    normalized_tokens = (unit_tokens * norm_gain_vector[None, :]).astype(jnp.bfloat16)
    joined_qkv = jnp.dot(normalized_tokens, w_qkv, preferred_element_type=jnp.float32)
    cos_table, sin_table = rope_tables(positions, HEAD)
    queries = rotate_pairs(joined_qkv[:, :query_cols].reshape(local_count, KVH, GROUP, HEAD), cos_table[:, None, None, :], sin_table[:, None, None, :]).astype(jnp.bfloat16)
    key_rows = rotate_pairs(joined_qkv[:, query_cols:query_cols + KVH * HEAD].reshape(local_count, KVH, HEAD), cos_table[:, None, :], sin_table[:, None, :]).astype(jnp.bfloat16)
    values = joined_qkv[:, query_cols + KVH * HEAD:].reshape(local_count, KVH, HEAD).astype(jnp.bfloat16)
    allowed = (doc_ids[:, None] == doc_ids[None, :]) & (positions[None, :] <= positions[:, None])
    score_scale = HEAD ** (-0.5)
    grad_heads = out_grad.reshape(local_count, KVH, GROUP, HEAD)

    def one_kv(kv_items):
        group_queries, kv_keys, kv_values, group_grads = kv_items

        def one_head(head_pair):
            head_query, head_grad = head_pair
            scores = jnp.dot(head_query, kv_keys.T, preferred_element_type=jnp.float32) * score_scale
            scores = jnp.where(allowed, scores, -jnp.inf)
            row_max = lax.optimization_barrier(jnp.max(scores, axis=1, keepdims=True))
            weights_exp = jnp.exp(scores - row_max)
            row_total = lax.optimization_barrier(jnp.sum(weights_exp, axis=1, keepdims=True))
            head_out = (jnp.dot(weights_exp.astype(jnp.bfloat16), kv_values, preferred_element_type=jnp.float32) / row_total).astype(jnp.bfloat16)
            log_total = row_max + jnp.log(row_total)
            row_delta = lax.optimization_barrier(jnp.sum(head_grad.astype(jnp.float32) * head_out.astype(jnp.float32), axis=1, keepdims=True))
            probability = jnp.exp(scores - log_total)
            d_value = jnp.dot(probability.astype(jnp.bfloat16).T, head_grad, preferred_element_type=jnp.float32)
            d_prob = jnp.dot(head_grad, kv_values.T, preferred_element_type=jnp.float32)
            d_score = (probability * (d_prob - row_delta) * score_scale).astype(jnp.bfloat16)
            d_query = jnp.dot(d_score, kv_keys, preferred_element_type=jnp.float32)
            d_key = jnp.dot(d_score.T, head_query, preferred_element_type=jnp.float32)
            return (head_out, d_query, d_key, d_value)
        head_out, d_query, d_key, d_value = lax.map(one_head, (group_queries, group_grads))
        return (head_out, d_query, lax.optimization_barrier(jnp.sum(d_key, axis=0)), lax.optimization_barrier(jnp.sum(d_value, axis=0)))
    head_out, d_query, d_key, d_value = lax.map(one_kv, (jnp.transpose(queries, (1, 2, 0, 3)), jnp.swapaxes(key_rows, 0, 1), jnp.swapaxes(values, 0, 1), jnp.transpose(grad_heads, (1, 2, 0, 3))))
    attended = jnp.transpose(head_out, (2, 0, 1, 3)).reshape(local_count, query_cols)
    d_query = rotate_pairs(jnp.transpose(d_query, (2, 0, 1, 3)), cos_table[:, None, None, :], -sin_table[:, None, None, :]).reshape(local_count, query_cols)
    d_key = rotate_pairs(jnp.swapaxes(d_key, 0, 1), cos_table[:, None, :], -sin_table[:, None, :]).reshape(local_count, KVH * HEAD)
    d_value = jnp.swapaxes(d_value, 0, 1).reshape(local_count, KVH * HEAD)
    d_joined = jnp.concatenate([d_query, d_key, d_value], axis=1).astype(jnp.bfloat16)
    normalized_grad = jnp.dot(d_joined, w_qkv.T, preferred_element_type=jnp.float32)
    w_term = jnp.dot(normalized_tokens.T, d_joined, preferred_element_type=jnp.float32)
    gain_product = lax.optimization_barrier(jnp.sum(normalized_grad * unit_tokens, axis=0))
    scaled_tokens = normalized_grad * norm_gain_vector[None, :]
    token_input_grad = (inverse_root * (scaled_tokens - unit_tokens * lax.optimization_barrier(jnp.mean(scaled_tokens * unit_tokens, axis=1, keepdims=True)))).astype(jnp.bfloat16)
    return (attended, token_input_grad, w_term, gain_product)

def reference(inputs, norm_gain_vector, w_qkv, doc_lengths, out_grad):

    def scan_step(state_now, episode_items):
        one_input, lengths, one_grad = episode_items
        attended, token_input_grad, w_term, gain_product = episode(one_input, lengths, one_grad, norm_gain_vector, w_qkv)
        return ((state_now[0] + w_term, state_now[1] + gain_product), (attended, token_input_grad))
    zero_sums = (jnp.zeros((D, KVH * (GROUP + 2) * HEAD), jnp.float32), jnp.zeros((D,), jnp.float32))
    (qkv_grad, gain_grad), (attended, token_input_grad) = lax.scan(scan_step, zero_sums, (inputs, doc_lengths, out_grad))
    attended = attended.reshape(EPIS, 2, N_CTX, HALF, KVH * GROUP * HEAD)
    inputs_grad = token_input_grad.reshape(EPIS, 2, N_CTX, HALF, D)
    return (attended, inputs_grad, qkv_grad, gain_grad)
```

```python
import functools

import jax
import jax.numpy as jnp
from jax import lax
from jax.experimental import pallas as pl
from jax.experimental.pallas import tpu as pltpu
from jax.sharding import Mesh
from jax.sharding import PartitionSpec as P

HEAD = 128
GROUP = 4
D = 2048
BLK = 128
TOK = 256
CHIP = 512
NBLK = 16
CHIPS = 4
WINDOW = 9
EPS = 1e-05
ROPE_BASE = 500000.0
SCALE = HEAD ** (-0.5)
F32, BF16 = jnp.float32, jnp.bfloat16
VMEM_LIMIT = 56 * 1024 * 1024

SPREAD1 = [(0, 2), (3, 1), (1, 0), (2, 3)]
SPREAD2 = [(1, 2), (2, 1)]
RETURN1 = [(2, 0), (1, 3), (0, 1), (3, 2)]
HOME_TO_VISITOR = [(0, 2), (3, 1)]
VISITOR_TO_HOME = [(2, 0), (1, 3)]
PAIR = ("c", "zl")


def params():
    return pltpu.CompilerParams(vmem_limit_bytes=VMEM_LIMIT)


def dot_nt(a, b):
    return lax.dot_general(a, b, (((1,), (1,)), ((), ())), preferred_element_type=F32)


def dot_tn(a, b):
    return lax.dot_general(a, b, (((0,), (0,)), ((), ())), preferred_element_type=F32)


def dot_nn(a, b):
    return lax.dot_general(a, b, (((1,), (0,)), ((), ())), preferred_element_type=F32)


def rotate(v, cos, sin):
    return v * cos + pltpu.roll(v, 64, 1) * sin


def kv_kernel(x_ref, gain_ref, w_ref, cos_ref, sin_ref, normed_ref, kv_ref):
    step = pl.program_id(0)

    @pl.when(step == 0)
    def _():
        x = x_ref[...].astype(F32)
        inv = lax.rsqrt(jnp.mean(x * x, axis=1, keepdims=True) + EPS)
        normed_ref[...] = ((x * inv) * gain_ref[...]).astype(BF16)

    out = dot_nn(normed_ref[...], w_ref[...])

    @pl.when(step < 2)
    def _():
        for i in range(2):
            cols = slice(i * HEAD, (i + 1) * HEAD)
            kv_ref[0, :, cols] = rotate(out[:, cols], cos_ref[...], sin_ref[...]).astype(BF16)

    @pl.when(step >= 2)
    def _():
        kv_ref[0] = out.astype(BF16)


def kv_call(x, gain, w, cos, sin):
    return pl.pallas_call(
        kv_kernel,
        grid=(4,),
        in_specs=[
            pl.BlockSpec((TOK, D), lambda t: (0, 0)),
            pl.BlockSpec((1, D), lambda t: (0, 0)),
            pl.BlockSpec((D, 256), lambda t: (0, 8 + t)),
            pl.BlockSpec((TOK, HEAD), lambda t: (0, 0)),
            pl.BlockSpec((TOK, HEAD), lambda t: (0, 0)),
        ],
        out_specs=[
            pl.BlockSpec((TOK, D), lambda t: (0, 0)),
            pl.BlockSpec((1, TOK, 256), lambda t: (t % 2, 0, t // 2)),
        ],
        out_shape=[
            jax.ShapeDtypeStruct((TOK, D), BF16),
            jax.ShapeDtypeStruct((2, TOK, 512), BF16),
        ],
        compiler_params=params(),
        cost_estimate=pl.CostEstimate(flops=2 * TOK * D * 1024, bytes_accessed=7 << 20, transcendentals=0),
        name="kv_home",
    )(x, gain, w, cos, sin)


def q_kernel(core_ref, n_ref, w_ref, cos_ref, sin_ref, q_ref):
    out = dot_nn(n_ref[...], w_ref[...])
    for i in range(2):
        cols = slice(i * HEAD, (i + 1) * HEAD)
        q_ref[:, cols] = rotate(out[:, cols], cos_ref[...], sin_ref[...]).astype(BF16)


def q_call(core, normed, w, cos, sin):
    return pl.pallas_call(
        q_kernel,
        grid_spec=pltpu.PrefetchScalarGridSpec(
            num_scalar_prefetch=1,
            grid=(4,),
            in_specs=[
                pl.BlockSpec((CHIP, D), lambda t, core: (0, 0)),
                pl.BlockSpec((D, 256), lambda t, core: (0, core[0] * 4 + t)),
                pl.BlockSpec((CHIP, HEAD), lambda t, core: (0, 0)),
                pl.BlockSpec((CHIP, HEAD), lambda t, core: (0, 0)),
            ],
            out_specs=pl.BlockSpec((CHIP, 256), lambda t, core: (0, t)),
        ),
        out_shape=jax.ShapeDtypeStruct((CHIP, 1024), BF16),
        compiler_params=params(),
        cost_estimate=pl.CostEstimate(flops=2 * CHIP * D * 1024, bytes_accessed=7 << 20, transcendentals=0),
        name="q_proj",
    )(core, normed, w, cos, sin)


def attention_kernel(
    where_ref, q_ref, do_ref, cos_ref, sin_ref, start_ref,
    s0, m0, s1, m1, s2, m2, s3, m3,
    o_ref, dq_ref, dkv_ref, kvbuf, acc, score,
):
    pieces = ((s0, m0), (s1, m1), (s2, m2), (s3, m3))
    for r in range(CHIPS):
        for part in range(2):
            for half in range(2):
                block = where_ref[8 + r * 4 + part * 2 + half]
                kvbuf[block] = pieces[r][part][half * BLK : (half + 1) * BLK, :]
    acc[...] = jnp.zeros_like(acc)
    row = lax.broadcasted_iota(jnp.int32, (BLK, GROUP * BLK), 0)
    for h in range(2):
        kc = slice(h * HEAD, (h + 1) * HEAD)
        vc = slice(256 + h * HEAD, 256 + (h + 1) * HEAD)
        for b in range(4):
            rows = slice(b * BLK, (b + 1) * BLK)
            heads = [slice((h * GROUP + g) * HEAD, (h * GROUP + g + 1) * HEAD) for g in range(GROUP)]
            queries = jnp.concatenate([q_ref[rows, g] for g in heads], axis=0)
            grads = jnp.concatenate([do_ref[rows, g] for g in heads], axis=0)
            block, first = where_ref[b], where_ref[4 + b]
            count = block - first + 1
            start = jnp.concatenate([start_ref[b]] * GROUP, axis=1)
            pos = block * BLK + lax.broadcasted_iota(jnp.int32, (1, GROUP * BLK), 1) % BLK

            def score_step(i, top, first=first, kc=kc, queries=queries, start=start, pos=pos):
                keys = kvbuf[first + i, :, kc]
                s = dot_nt(keys, queries) * SCALE
                at = (first + i) * BLK + row
                s = jnp.where((at >= start) & (at <= pos), s, -jnp.inf)
                score[i] = s
                return jnp.maximum(top, jnp.max(s.reshape(BLK // 8, 8, GROUP * BLK), axis=0))

            top = lax.fori_loop(0, count, score_step, jnp.full((8, GROUP * BLK), -jnp.inf, F32))
            top = jnp.max(top, axis=0, keepdims=True)

            def value_step(i, carry, first=first, vc=vc, top=top):
                total, out = carry
                e = jnp.exp(score[i] - top)
                score[i] = e
                total = total + jnp.sum(e.reshape(BLK // 8, 8, GROUP * BLK), axis=0)
                out = out + dot_tn(kvbuf[first + i, :, vc], e.astype(BF16))
                return total, out

            total, out = lax.fori_loop(
                0, count, value_step,
                (jnp.zeros((8, GROUP * BLK), F32), jnp.zeros((HEAD, GROUP * BLK), F32)),
            )
            inv = 1.0 / jnp.sum(total, axis=0, keepdims=True)
            out = (out * inv).astype(BF16).astype(F32)
            delta = jnp.sum(out * grads.astype(F32).T, axis=0, keepdims=True)
            for g in range(GROUP):
                o_ref[rows, heads[g]] = out[:, g * BLK : (g + 1) * BLK].T.astype(BF16)

            def grad_step(i, dq, first=first, kc=kc, vc=vc, inv=inv, delta=delta, queries=queries, grads=grads):
                keys, values = kvbuf[first + i, :, kc], kvbuf[first + i, :, vc]
                p = score[i] * inv
                dp = dot_nt(values, grads)
                ds = (p * (dp - delta) * SCALE).astype(BF16)
                acc[first + i, :, vc] += dot_nn(p.astype(BF16), grads)
                acc[first + i, :, kc] += dot_nn(ds, queries)
                return dq + dot_tn(keys, ds)

            dq = lax.fori_loop(0, count, grad_step, jnp.zeros((HEAD, GROUP * BLK), F32))
            cos, sin = cos_ref[rows, :], sin_ref[rows, :]
            for g in range(GROUP):
                part = dq[:, g * BLK : (g + 1) * BLK].T
                dq_ref[rows, heads[g]] = rotate(part, cos, -sin).astype(BF16)
    for r in range(CHIPS):
        for j in range(4):
            dkv_ref[r, j * BLK : (j + 1) * BLK, :] = acc[where_ref[8 + r * 4 + j]].astype(BF16)


def attention_call(where, q, do, cos, sin, start, pieces):
    vmem = pl.BlockSpec(memory_space=pltpu.VMEM)
    return pl.pallas_call(
        attention_kernel,
        in_specs=[pl.BlockSpec(memory_space=pltpu.SMEM)] + [vmem] * (5 + len(pieces)),
        out_specs=[vmem] * 3,
        out_shape=[
            jax.ShapeDtypeStruct((CHIP, 1024), BF16),
            jax.ShapeDtypeStruct((CHIP, 1024), BF16),
            jax.ShapeDtypeStruct((CHIPS, CHIP, 512), BF16),
        ],
        scratch_shapes=[
            pltpu.VMEM((NBLK, BLK, 512), BF16),
            pltpu.VMEM((NBLK, BLK, 512), F32),
            pltpu.VMEM((WINDOW, BLK, GROUP * BLK), F32),
        ],
        compiler_params=params(),
        cost_estimate=pl.CostEstimate(flops=12 * CHIP * 1024 * 1152, bytes_accessed=10 << 20, transcendentals=8 << 20),
        name="attention",
    )(where, q, do, cos, sin, start, *pieces)


def joined_kernel(a, b, c, d, cos_ref, sin_ref, out_ref):
    total = a[...].astype(F32) + b[...].astype(F32) + c[...].astype(F32) + d[...].astype(F32)
    for i in range(2):
        cols = slice(i * HEAD, (i + 1) * HEAD)
        out_ref[:, cols] = rotate(total[:, cols], cos_ref[...], -sin_ref[...]).astype(BF16)
    out_ref[:, 256:] = total[:, 256:].astype(BF16)


def joined_call(own, others, cos, sin):
    vmem = pl.BlockSpec(memory_space=pltpu.VMEM)
    return pl.pallas_call(
        joined_kernel,
        in_specs=[vmem] * 6,
        out_specs=vmem,
        out_shape=jax.ShapeDtypeStruct((CHIP, 512), BF16),
        compiler_params=params(),
        cost_estimate=pl.CostEstimate(flops=1 << 20, bytes_accessed=3 << 20, transcendentals=0),
        name="joined_kv",
    )(own, *others, cos, sin)


def dnorm_kernel(core_ref, jq_ref, jkv_ref, wq_ref, wk_ref, wv_ref, out_ref):
    out = dot_nt(jq_ref[...], wq_ref[...])
    out += dot_nt(jkv_ref[:, :256], wk_ref[...])
    out += dot_nt(jkv_ref[:, 256:], wv_ref[...])
    out_ref[0] = out[:TOK].astype(BF16)
    out_ref[1] = out[TOK:].astype(BF16)


def dnorm_call(core, jq, jkv, w):
    tile = 512
    return pl.pallas_call(
        dnorm_kernel,
        grid_spec=pltpu.PrefetchScalarGridSpec(
            num_scalar_prefetch=1,
            grid=(D // tile,),
            in_specs=[
                pl.BlockSpec((CHIP, 1024), lambda t, core: (0, 0)),
                pl.BlockSpec((CHIP, 512), lambda t, core: (0, 0)),
                pl.BlockSpec((tile, 1024), lambda t, core: (t, core[0])),
                pl.BlockSpec((tile, 256), lambda t, core: (t, 8 + core[0])),
                pl.BlockSpec((tile, 256), lambda t, core: (t, 10 + core[0])),
            ],
            out_specs=pl.BlockSpec((2, TOK, tile), lambda t, core: (0, 0, t)),
        ),
        out_shape=jax.ShapeDtypeStruct((2, TOK, D), BF16),
        compiler_params=params(),
        cost_estimate=pl.CostEstimate(flops=2 * CHIP * D * 1536, bytes_accessed=11 << 20, transcendentals=0),
        name="d_normed",
    )(core, jq, jkv, w, w, w)


def weight_kernel(core_ref, n0, d1, d2, d3, v1, v2, v3, jq0, jq1, jq2, jq3, jkv0, jkv1, jkv2, jkv3, out_ref):
    core = core_ref[0]
    near, far = pl.ds(core * TOK, TOK), pl.ds((1 - core) * TOK, TOK)
    for js, cols in (((jq0, jq1, jq2, jq3), slice(0, 256)), ((jkv0, jkv1, jkv2, jkv3), slice(256, 384))):
        out = dot_tn(n0[...], js[0][...])
        for direct, via, j in ((d1, v1, js[1]), (d2, v2, js[2]), (d3, v3, js[3])):
            out += dot_tn(direct[...], j[near, :])
            out += dot_tn(via[...], j[far, :])
        out = out.astype(BF16)
        for i in range(2):
            for k in range(8):
                at = i * 128 + k * 16
                out_ref[0, k, i, :, cols] = out[at : at + 16]


def weight_call(core, own, direct, via, jq, jkv):
    tile = 256
    part = pl.BlockSpec((TOK, tile), lambda t, core: (0, t))
    return pl.pallas_call(
        weight_kernel,
        grid_spec=pltpu.PrefetchScalarGridSpec(
            num_scalar_prefetch=1,
            grid=(D // tile,),
            in_specs=[pl.BlockSpec((CHIP, tile), lambda t, core: (0, t))]
            + [part] * 6
            + [pl.BlockSpec((CHIP, 256), lambda t, core: (0, 0))] * 4
            + [pl.BlockSpec((CHIP, 128), lambda t, core: (0, 0))] * 4,
            out_specs=pl.BlockSpec((1, 8, 2, 16, 384), lambda t, core: (t, 0, 0, 0, 0)),
        ),
        out_shape=jax.ShapeDtypeStruct((8, 8, 2, 16, 384), BF16),
        compiler_params=params(),
        cost_estimate=pl.CostEstimate(flops=2 * D * D * 384, bytes_accessed=12 << 20, transcendentals=0),
        name="weight_grad",
    )(core, own, *direct, *via, *jq, *jkv)


def shift(value, axis, by):
    return lax.ppermute(value, axis, [(i, (i + by) % 4) for i in range(4)])


def positions_of(ctx):
    offset = jnp.arange(BLK, dtype=jnp.int32)
    return jnp.concatenate([ctx * BLK + offset, (15 - ctx) * BLK + offset])


def body(inputs, gain, w, doc_lengths, out_grad):
    c, zl, y, x_at, zh = (lax.axis_index(a) for a in ("c", "zl", "y", "x", "zh"))
    resident = c == zl
    core = c.astype(jnp.int32).reshape(1)
    x = inputs.reshape(TOK, D)
    grads = out_grad.reshape(TOK, 2048)

    near, far = 2 * y + zl, 2 * y + 1 - zl
    positions = jnp.concatenate([positions_of(near), positions_of(far)])
    frequency = jnp.power(jnp.float32(ROPE_BASE), -2.0 * jnp.arange(64, dtype=F32) / HEAD)
    angles = positions.astype(F32)[:, None] * frequency[None, :]
    cos, sin = jnp.cos(angles), jnp.sin(angles)
    cos = jnp.concatenate([cos, cos], axis=1)
    sin = jnp.concatenate([-sin, sin], axis=1)

    normed, kv = kv_call(x, gain.reshape(1, D), w, cos[:TOK], sin[:TOK])

    kv_mine = lax.dynamic_index_in_dim(kv, zl, 0, keepdims=False)
    kv_other = lax.dynamic_index_in_dim(kv, 1 - zl, 0, keepdims=False)
    r1 = lax.ppermute(kv_other, PAIR, SPREAD1)
    r2 = lax.ppermute(kv_mine, PAIR, SPREAD2)
    kv_s = jnp.where(resident, kv_mine, r1)
    kv_m = jnp.where(resident, r1, r2)
    pieces = [kv_s, kv_m]
    back = {}
    for by in (2, 1, 3):
        back[(4 - by) % 4] = (shift(kv_s, "y", by), shift(kv_m, "y", by))
    for r in (1, 2, 3):
        pieces += list(back[r])

    n1 = lax.ppermute(normed, PAIR, HOME_TO_VISITOR)
    n2 = lax.ppermute(normed, PAIR, SPREAD2)
    n3 = lax.ppermute(n2, PAIR, VISITOR_TO_HOME)
    normed_all = jnp.concatenate([jnp.where(resident, normed, n1), jnp.where(resident, n3, n2)], axis=0)

    g_halves = grads.reshape(TOK, 2, 1024)
    g_mine = lax.dynamic_index_in_dim(g_halves, zl, 1, keepdims=False)
    g_other = lax.dynamic_index_in_dim(g_halves, 1 - zl, 1, keepdims=False)
    g1 = lax.ppermute(g_other, PAIR, SPREAD1)
    g2 = lax.ppermute(g_mine, PAIR, SPREAD2)
    do_all = jnp.concatenate([jnp.where(resident, g_mine, g1), jnp.where(resident, g1, g2)], axis=0)

    lengths = doc_lengths.reshape(16)
    lengths = jnp.where(resident, lengths, lax.ppermute(lengths, PAIR, HOME_TO_VISITOR))
    upto = jnp.arange(16)
    ends = jnp.sum(jnp.where(upto[None, :] <= upto[:, None], lengths[None, :], 0), axis=1)
    start = jnp.max(jnp.where(positions[:, None] >= ends[None, :], ends[None, :], 0), axis=1).astype(jnp.int32)
    start = start.reshape(4, 1, BLK)
    blocks = []
    for r in range(CHIPS):
        a, b = 2 * ((y + r) % 4) + zl, 2 * ((y + r) % 4) + 1 - zl
        blocks += [a, 15 - a, b, 15 - b]
    blocks = jnp.stack(blocks).astype(jnp.int32)
    where = jnp.concatenate([blocks[:4], start[:, 0, 0] // BLK, blocks])

    mine = lax.dynamic_slice_in_dim(normed_all, c * TOK, TOK, 0)
    direct = {(4 - by) % 4: shift(mine, "x", by) for by in (2, 1, 3)}
    via = {r: lax.ppermute(direct[r], "c", [(0, 1), (1, 0)]) for r in (1, 2, 3)}

    q = q_call(core, normed_all, w, cos, sin)
    o, dq, dkv = attention_call(where, q, do_all, cos, sin, start, pieces)

    def to_x(value, width):
        parts = value.reshape(CHIP, 4, width)
        pick = lambda r: lax.dynamic_index_in_dim(parts, (x_at + r) % 4, 1, keepdims=False)
        got = {(4 - by) % 4: shift(pick(by), "x", by) for by in (2, 1, 3)}
        return [pick(0), got[1], got[2], got[3]]

    others = [shift(dkv[by], "y", by) for by in (2, 1, 3)]
    jq = to_x(dq, 256)

    o_s, o_m = o[:TOK], o[TOK:]
    h1 = lax.ppermute(jnp.where(resident, o_m, o_s), PAIR, RETURN1)
    h2 = lax.ppermute(o_m, PAIR, SPREAD2)
    half_mine = jnp.where(resident, o_s, h2)
    attended = jnp.where(
        zl == 0, jnp.concatenate([half_mine, h1], axis=1), jnp.concatenate([h1, half_mine], axis=1)
    )

    joined_kv = joined_call(dkv[0], others, cos, sin)
    jkv = to_x(joined_kv, 128)

    dn = dnorm_call(core, dq, joined_kv, w)
    dn_s, dn_m = dn[0], dn[1]
    d1 = lax.ppermute(jnp.where(resident, dn_m, dn_s), "c", [(0, 1), (1, 0)])
    summed = jnp.where(resident, dn_s, dn_m).astype(F32) + d1.astype(F32)
    d2 = lax.ppermute(summed.astype(BF16), PAIR, SPREAD2)
    d_normed = jnp.where(resident, summed, d2.astype(F32))

    wg = weight_call(core, normed_all, [direct[r] for r in (1, 2, 3)], [via[r] for r in (1, 2, 3)], jq, jkv)
    wg = lax.all_to_all(wg.reshape(64, 2, 16, 384), ("x", "zh", "y", "zl"), 0, 0, tiled=True)
    wg = jnp.sum(wg.reshape(4, 16, 2, 16, 384).astype(F32), axis=1)
    keep = lax.dynamic_index_in_dim(wg, c, 1, keepdims=False)
    give = lax.dynamic_index_in_dim(wg, 1 - c, 1, keepdims=False)
    got = lax.ppermute(give, "c", [(0, 1), (1, 0)])
    first, second = jnp.where(c == 0, keep, got), jnp.where(c == 0, got, keep)
    both = jnp.stack([first, second])
    gq = both[..., :256].transpose(2, 0, 1, 3).reshape(16, 2048)
    gkv = both[..., 256:].reshape(2, 2, 2, 16, HEAD)
    gkv = gkv.transpose(3, 1, 0, 2, 4).reshape(16, 1024)
    qkv_grad = jnp.concatenate([gq, gkv], axis=1)

    at = ((((x_at * 2 + zh) * 2 + c) * 4 + y) * 2 + zl) * 16
    w_rows = lax.dynamic_slice_in_dim(w, at, 16, 0).astype(F32)
    gain_grad = jnp.sum(w_rows * qkv_grad, axis=1) / lax.dynamic_slice_in_dim(gain, at, 16, 0)

    xf = x.astype(F32)
    inv = lax.rsqrt(jnp.mean(xf * xf, axis=1, keepdims=True) + EPS)
    unit = xf * inv
    scaled = d_normed * gain[None, :]
    inputs_grad = (inv * (scaled - unit * jnp.mean(scaled * unit, axis=1, keepdims=True))).astype(BF16)
    return (
        attended.reshape(1, 2, 1, BLK, 2048),
        inputs_grad.reshape(1, 2, 1, BLK, D),
        qkv_grad,
        gain_grad,
    )


def solution(mesh):
    fine = Mesh(mesh.devices.reshape(4, 2, 2, 4, 2), ("x", "zh", "c", "y", "zl"))
    dp, ctx = ("x", "zh", "c"), ("y", "zl")
    rows = P(dp, None, ctx, None, None)
    return jax.shard_map(
        body,
        mesh=fine,
        in_specs=(rows, P(), P(), P(dp, None), rows),
        out_specs=(rows, rows, P(dp + ctx, None), P(dp + ctx)),
        check_vma=False,
    )
```

```python
import jax
import jax.numpy as jnp
import numpy as np
from jax import lax
from jax.experimental import pallas as pl
from jax.experimental.pallas import tpu as pltpu
from jax.sharding import Mesh
from jax.sharding import PartitionSpec as P

HEAD = 128
GROUP = 4
D = 2048
BLK = 128
TOK = 256
CHIP = 512
NBLK = 16
WCOLS = 384
CHIPS = 4
PAIR_TOK = 2 * BLK
COLS = 4 * PAIR_TOK
WINDOW = 5
EPS = 1e-05
ROPE_BASE = 500000.0
SCALE = HEAD ** (-0.5)
EXP2_SCALE = SCALE * 1.4426950408889634
F32, BF16 = jnp.float32, jnp.bfloat16
VMEM_LIMIT = 56 * 1024 * 1024

ANGLES = np.arange(2048)[:, None] * ROPE_BASE ** (-2.0 * np.arange(64) / HEAD)
TABLE = np.concatenate([np.cos(ANGLES)] * 2 + [-np.sin(ANGLES), np.sin(ANGLES)], axis=1).astype(np.float32)

SPREAD1 = [(0, 2), (3, 1), (1, 0), (2, 3)]
SPREAD2 = [(1, 2), (2, 1)]
RETURN1 = [(2, 0), (1, 3), (0, 1), (3, 2)]
HOME_TO_VISITOR = [(0, 2), (3, 1)]
VISITOR_ACROSS = [(1, 0), (2, 3)]
PAIR = ("c", "zl")


def cost(us):
    return pl.CostEstimate(flops=int(us * 10**6), bytes_accessed=int(us * (1 << 20)), transcendentals=0)


def params():
    return pltpu.CompilerParams(vmem_limit_bytes=VMEM_LIMIT)


def dot_nt(a, b):
    return lax.dot_general(a, b, (((1,), (1,)), ((), ())), preferred_element_type=F32)


def dot_tn(a, b):
    return lax.dot_general(a, b, (((0,), (0,)), ((), ())), preferred_element_type=F32)


def dot_nn(a, b):
    return lax.dot_general(a, b, (((1,), (0,)), ((), ())), preferred_element_type=F32)


def rotate(v, cos, sin):
    return v * cos + pltpu.roll(v, 64, 1) * sin


def kv_kernel(sel_ref, x_ref, gain_ref, wk_ref, wv_ref, ta_ref, tb_ref, normed_ref, mine_ref, other_ref):
    step = pl.program_id(0)

    @pl.when(step == 0)
    def _():
        x = x_ref[...].astype(F32)
        inv = lax.rsqrt(jnp.mean(x * x, axis=1, keepdims=True) + EPS)
        normed_ref[...] = ((x * inv) * gain_ref[...]).astype(BF16)

    keys = dot_nn(normed_ref[...], wk_ref[...])
    values = dot_nn(normed_ref[...], wv_ref[...]).astype(BF16)
    table = jnp.concatenate([ta_ref[...], tb_ref[...]], axis=0)
    cos, sin = table[:, :HEAD], table[:, HEAD:]
    keys = jnp.concatenate(
        [rotate(keys[:, i * HEAD : (i + 1) * HEAD], cos, sin).astype(BF16) for i in range(2)], axis=1
    )

    @pl.when(step == 0)
    def _():
        mine_ref[:, :256] = keys
        mine_ref[:, 256:] = values

    @pl.when(step == 1)
    def _():
        other_ref[:, :256] = keys
        other_ref[:, 256:] = values


def kv_call(sel, x, gain, w, table):
    half = jax.ShapeDtypeStruct((TOK, 512), BF16)
    return pl.pallas_call(
        kv_kernel,
        grid_spec=pltpu.PrefetchScalarGridSpec(
            num_scalar_prefetch=1,
            grid=(2,),
            in_specs=[
                pl.BlockSpec((TOK, D), lambda t, sel: (0, 0)),
                pl.BlockSpec((1, D), lambda t, sel: (0, 0)),
                pl.BlockSpec((D, 256), lambda t, sel: (0, 8 + (sel[0] + t) % 2)),
                pl.BlockSpec((D, 256), lambda t, sel: (0, 10 + (sel[0] + t) % 2)),
                pl.BlockSpec((BLK, 256), lambda t, sel: (sel[1], 0)),
                pl.BlockSpec((BLK, 256), lambda t, sel: (sel[2], 0)),
            ],
            out_specs=[
                pl.BlockSpec((TOK, D), lambda t, sel: (0, 0)),
                pl.BlockSpec((TOK, 512), lambda t, sel: (0, 0)),
                pl.BlockSpec((TOK, 512), lambda t, sel: (0, 0)),
            ],
        ),
        out_shape=[jax.ShapeDtypeStruct((TOK, D), BF16), half, half],
        compiler_params=params(),
        cost_estimate=cost(0.01),
        name="kv_home",
    )(sel, x, gain, w, w, table, table)


def q_kernel(sel_ref, n_ref, w_ref, ta_ref, tb_ref, q_ref):
    out = dot_nn(n_ref[...], w_ref[...])
    table = jnp.concatenate([ta_ref[...], tb_ref[...]], axis=0)
    for i in range(4):
        cols = slice(i * HEAD, (i + 1) * HEAD)
        q_ref[:, cols] = rotate(out[:, cols], table[:, :HEAD], table[:, HEAD:]).astype(BF16)


def q_call(sel, normed, w, table):
    return pl.pallas_call(
        q_kernel,
        grid_spec=pltpu.PrefetchScalarGridSpec(
            num_scalar_prefetch=1,
            grid=(2,),
            in_specs=[
                pl.BlockSpec((TOK, D), lambda t, sel: (0, 0)),
                pl.BlockSpec((D, 512), lambda t, sel: (0, sel[0] * 2 + t)),
                pl.BlockSpec((BLK, 256), lambda t, sel: (sel[1], 0)),
                pl.BlockSpec((BLK, 256), lambda t, sel: (sel[2], 0)),
            ],
            out_specs=pl.BlockSpec((TOK, 512), lambda t, sel: (0, t)),
        ),
        out_shape=jax.ShapeDtypeStruct((TOK, 1024), BF16),
        compiler_params=params(),
        cost_estimate=cost(4),
        name="q_proj",
    )(sel, normed, w, table, table)


def attention_kernel(
    where_ref, qs_ref, qm_ref, dos_ref, dom_ref, table_ref, start_ref, kv0, kv1, kv2, kv3,
    keep_ref, give_ref, dq_ref, x0, x1, x2, x3, t0, t1, t2, t3, kvbuf, acc, score, quarters,
):
    pieces = (kv0, kv1, kv2, kv3)
    home = where_ref[7] == 0
    for r in range(CHIPS):
        for part in range(2):
            for half in range(2):
                block = where_ref[8 + r * 4 + part * 2 + half]
                kvbuf[block] = pieces[r][part, half * BLK : (half + 1) * BLK, :]
    acc[...] = jnp.zeros_like(acc)
    row = lax.broadcasted_iota(jnp.int32, (PAIR_TOK, COLS), 0)
    for p in range(2):
        rows = slice(p * BLK, (p + 1) * BLK)
        heads = [[slice((h * GROUP + g) * HEAD, (h * GROUP + g + 1) * HEAD) for g in range(GROUP)] for h in range(2)]
        kc = [slice(h * HEAD, (h + 1) * HEAD) for h in range(2)]
        vc = [slice(256 + h * HEAD, 256 + (h + 1) * HEAD) for h in range(2)]
        queries = [jnp.concatenate([ref[rows, g] for ref in (qs_ref, qm_ref) for g in heads[h]], axis=0) for h in range(2)]
        grads = [jnp.concatenate([ref[rows, g] for ref in (dos_ref, dom_ref) for g in heads[h]], axis=0) for h in range(2)]
        first = where_ref[4 + p]
        count = where_ref[p] // 2 - first + 1
        start = jnp.concatenate([start_ref[p]] * GROUP + [start_ref[2 + p]] * GROUP, axis=1)
        token = lax.broadcasted_iota(jnp.int32, (1, GROUP * BLK), 1) % BLK
        pos = jnp.concatenate([where_ref[p] * BLK + token, where_ref[2 + p] * BLK + token], axis=1)

        def pair(i, cols):
            return jnp.concatenate([kvbuf[2 * i, :, cols], kvbuf[2 * i + 1, :, cols]], axis=0)

        def score_step(i, tops, first=first, kc=kc, queries=queries, start=start, pos=pos):
            at = (first + i) * PAIR_TOK + row
            allowed = (at >= start) & (at <= pos)
            out = []
            for h in range(2):
                s = dot_nt(pair(first + i, kc[h]), queries[h])
                s = jnp.where(allowed, s, -jnp.inf)
                score[h, i] = s
                out.append(jnp.maximum(tops[h], jnp.max(s.reshape(PAIR_TOK // 8, 8, COLS), axis=0)))
            return tuple(out)

        tops = lax.fori_loop(0, count, score_step, (jnp.full((8, COLS), -jnp.inf, F32),) * 2)
        tops = [jnp.max(t, axis=0, keepdims=True) * EXP2_SCALE for t in tops]

        def value_step(i, carry, first=first, vc=vc, tops=tops):
            res = []
            for h in range(2):
                total, out = carry[h]
                e = jnp.exp2(score[h, i] * EXP2_SCALE - tops[h])
                score[h, i] = e
                total = total + jnp.sum(e.reshape(PAIR_TOK // 8, 8, COLS), axis=0)
                out = out + dot_tn(pair(first + i, vc[h]), e.astype(BF16))
                res.append((total, out))
            return tuple(res)

        carry = lax.fori_loop(
            0, count, value_step, ((jnp.zeros((8, COLS), F32), jnp.zeros((HEAD, COLS), F32)),) * 2
        )
        invs, deltas = [], []
        for h in range(2):
            total, out = carry[h]
            inv = 1.0 / jnp.sum(total, axis=0, keepdims=True)
            out = (out * inv).astype(BF16).astype(F32)
            deltas.append(jnp.sum(out * grads[h].astype(F32).T, axis=0, keepdims=True))
            invs.append(inv)
            for g in range(GROUP):
                of_s = out[:, g * BLK : (g + 1) * BLK].T.astype(BF16)
                of_m = out[:, (GROUP + g) * BLK : (GROUP + g + 1) * BLK].T.astype(BF16)
                keep_ref[rows, heads[h][g]] = jnp.where(home, of_s, of_m)
                give_ref[rows, heads[h][g]] = jnp.where(home, of_m, of_s)

        def grad_step(i, dqs, first=first, kc=kc, vc=vc, invs=invs, deltas=deltas, queries=queries, grads=grads):
            res = []
            j = first + i
            for h in range(2):
                keys, values = pair(j, kc[h]), pair(j, vc[h])
                prob = score[h, i] * invs[h]
                dp = dot_nt(values, grads[h])
                ds = (prob * (dp - deltas[h])).astype(BF16)
                dv = dot_nn(prob.astype(BF16), grads[h])
                dk = dot_nn(ds, queries[h])
                for k in range(2):
                    acc[2 * j + k, :, vc[h]] += dv[k * BLK : (k + 1) * BLK]
                    acc[2 * j + k, :, kc[h]] += dk[k * BLK : (k + 1) * BLK]
                res.append(dqs[h] + dot_tn(keys, ds))
            return tuple(res)

        dqs = lax.fori_loop(0, count, grad_step, (jnp.zeros((HEAD, COLS), F32),) * 2)
        for k in range(2):
            at = (2 * k + p) * BLK
            rows = slice(at, at + BLK)
            cos, sin = table_ref[rows, :HEAD] * SCALE, table_ref[rows, HEAD:] * SCALE
            for h in range(2):
                for g in range(GROUP):
                    at = (k * GROUP + g) * BLK
                    part = rotate(dqs[h][:, at : at + BLK].T, cos, -sin).astype(BF16)
                    dq_ref[rows, heads[h][g]] = part
                    j = h * GROUP + g
                    quarters[j // 2, rows, (j % 2) * HEAD : (j % 2 + 1) * HEAD] = part
    for r, out in enumerate((x0, x1, x2, x3)):
        out[...] = quarters[(where_ref[6] + r) % 4]
    for r, out in enumerate((t0, t1, t2, t3)):
        for j in range(4):
            at, rows = where_ref[8 + r * 4 + j], slice(j * BLK, (j + 1) * BLK)
            out[rows, :256] = (acc[at, :, :256] * SCALE).astype(BF16)
            out[rows, 256:] = acc[at, :, 256:].astype(BF16)


def attention_call(where, q, do, table, start, pieces):
    vmem = pl.BlockSpec(memory_space=pltpu.VMEM)
    half = jax.ShapeDtypeStruct((TOK, 1024), BF16)
    out = pl.pallas_call(
        attention_kernel,
        in_specs=[pl.BlockSpec(memory_space=pltpu.SMEM)] + [vmem] * 10,
        out_specs=[vmem] * 11,
        out_shape=[half, half, jax.ShapeDtypeStruct((CHIP, 1024), BF16)]
        + [jax.ShapeDtypeStruct((CHIP, 256), BF16)] * 4
        + [jax.ShapeDtypeStruct((CHIP, 512), BF16)] * 4,
        scratch_shapes=[
            pltpu.VMEM((NBLK, BLK, 512), BF16),
            pltpu.VMEM((NBLK, BLK, 512), F32),
            pltpu.VMEM((2, WINDOW, PAIR_TOK, COLS), F32),
            pltpu.VMEM((4, CHIP, 256), BF16),
        ],
        compiler_params=params(),
        cost_estimate=cost(0.1),
        name="attention",
    )(where, *q, *do, table, start, *pieces)
    return out[0], out[1], out[2], out[3:7], out[7:]


def joined_kernel(x_ref, a, b, c, d, table_ref, out_ref, j0, j1, j2, j3):
    total = a[...].astype(F32) + b[...].astype(F32) + c[...].astype(F32) + d[...].astype(F32)
    for i in range(2):
        cols = slice(i * HEAD, (i + 1) * HEAD)
        out_ref[:, cols] = rotate(total[:, cols], table_ref[:, :HEAD], -table_ref[:, HEAD:]).astype(BF16)
    out_ref[:, 256:] = total[:, 256:].astype(BF16)
    for r, out in enumerate((j0, j1, j2, j3)):
        out[...] = out_ref[:, pl.ds(pl.multiple_of((x_ref[0] + r) % 4 * HEAD, HEAD), HEAD)]


def joined_call(x_at, own, others, table):
    vmem = pl.BlockSpec(memory_space=pltpu.VMEM)
    out = pl.pallas_call(
        joined_kernel,
        in_specs=[pl.BlockSpec(memory_space=pltpu.SMEM)] + [vmem] * 5,
        out_specs=[vmem] * 5,
        out_shape=[jax.ShapeDtypeStruct((CHIP, 512), BF16)] + [jax.ShapeDtypeStruct((CHIP, HEAD), BF16)] * 4,
        compiler_params=params(),
        cost_estimate=cost(0.1),
        name="joined_kv",
    )(x_at, own, *others, table)
    return out[0], out[1:]


def dnorm_q_kernel(sel_ref, j_ref, w_ref, out_ref):
    out_ref[...] = dot_nt(j_ref[...], w_ref[...]).astype(BF16)


def dnorm_q_call(sel, jq, w):
    tile = 512
    return pl.pallas_call(
        dnorm_q_kernel,
        grid_spec=pltpu.PrefetchScalarGridSpec(
            num_scalar_prefetch=1,
            grid=(D // tile,),
            in_specs=[
                pl.BlockSpec((CHIP, 1024), lambda t, sel: (0, 0)),
                pl.BlockSpec((tile, 1024), lambda t, sel: (t, sel[0])),
            ],
            out_specs=pl.BlockSpec((CHIP, tile), lambda t, sel: (0, t)),
        ),
        out_shape=jax.ShapeDtypeStruct((CHIP, D), BF16),
        compiler_params=params(),
        cost_estimate=cost(6),
        name="d_normed_q",
    )(sel, jq, w)


def dnorm_kernel(sel_ref, part_ref, jkv_ref, wk_ref, wv_ref, keep_ref, give_ref):
    out = part_ref[...].astype(F32)
    out += dot_nt(jkv_ref[:, :256], wk_ref[...])
    out += dot_nt(jkv_ref[:, 256:], wv_ref[...])
    home = sel_ref[1] == 0
    of_s, of_m = out[:TOK].astype(BF16), out[TOK:].astype(BF16)
    keep_ref[...] = jnp.where(home, of_s, of_m)
    give_ref[...] = jnp.where(home, of_m, of_s)


def dnorm_call(sel, part, jkv, w):
    tile = 1024
    return pl.pallas_call(
        dnorm_kernel,
        grid_spec=pltpu.PrefetchScalarGridSpec(
            num_scalar_prefetch=1,
            grid=(D // tile,),
            in_specs=[
                pl.BlockSpec((CHIP, tile), lambda t, sel: (0, t)),
                pl.BlockSpec((CHIP, 512), lambda t, sel: (0, 0)),
                pl.BlockSpec((tile, 256), lambda t, sel: (t, 8 + sel[0])),
                pl.BlockSpec((tile, 256), lambda t, sel: (t, 10 + sel[0])),
            ],
            out_specs=[pl.BlockSpec((TOK, tile), lambda t, sel: (0, t))] * 2,
        ),
        out_shape=[jax.ShapeDtypeStruct((TOK, D), BF16)] * 2,
        compiler_params=params(),
        cost_estimate=cost(3),
        name="d_normed",
    )(sel, part, jkv, w, w)


def weight_kernel(sel_ref, ns, nm, d1, d2, d3, v1, v2, v3, q0, q1, q2, q3, k0, k1, k2, k3, out_ref, jt):
    role = sel_ref[1]
    pieces = ((ns, q0, k0, 0), (nm, q0, k0, TOK))
    for direct, via, q, k in ((d1, v1, q1, k1), (d2, v2, q2, k2), (d3, v3, q3, k3)):
        pieces += ((direct, q, k, role * TOK), (via, q, k, (1 - role) * TOK))

    @pl.when(pl.program_id(0) == 0)
    def _():
        for i, (_, q, k, at) in enumerate(pieces):
            jt[:256, i * TOK : (i + 1) * TOK] = q[pl.ds(at, TOK), :].T
            jt[256:, i * TOK : (i + 1) * TOK] = k[pl.ds(at, TOK), :].T

    out = jnp.zeros((WCOLS, out_ref.shape[0] * TOK), F32)
    for i, (n, _, _, _) in enumerate(pieces):
        out += dot_nn(jt[:, i * TOK : (i + 1) * TOK], n[...])
    for t in range(out_ref.shape[0]):
        part = out[:, t * TOK : (t + 1) * TOK].T.astype(BF16)
        for i in range(2):
            for k in range(8):
                at = i * 128 + k * 16
                out_ref[t, k, i] = part[at : at + 16]


def weight_call(sel, tokens, direct, via, jq, jkv):
    tile = 512
    part = pl.BlockSpec((TOK, tile), lambda t, sel: (0, t))
    return pl.pallas_call(
        weight_kernel,
        grid_spec=pltpu.PrefetchScalarGridSpec(
            num_scalar_prefetch=1,
            grid=(D // tile,),
            in_specs=[part] * 8
            + [pl.BlockSpec((CHIP, 256), lambda t, sel: (0, 0))] * 4
            + [pl.BlockSpec((CHIP, HEAD), lambda t, sel: (0, 0))] * 4,
            out_specs=pl.BlockSpec((tile // TOK, 8, 2, 16, WCOLS), lambda t, sel: (t, 0, 0, 0, 0)),
            scratch_shapes=[pltpu.VMEM((WCOLS, 8 * TOK), BF16)],
        ),
        out_shape=jax.ShapeDtypeStruct((8, 8, 2, 16, WCOLS), BF16),
        compiler_params=params(),
        cost_estimate=cost(0.1),
        name="weight_grad",
    )(sel, *tokens, *direct, *via, *jq, *jkv)


def sum_kernel(sel_ref, parts_ref, keep_ref, give_ref):
    core = sel_ref[0]
    for x in range(4):
        keep_ref[x] = jnp.sum(parts_ref[x * 16 : (x + 1) * 16, core].astype(F32), axis=0)
        give_ref[x] = jnp.sum(parts_ref[x * 16 : (x + 1) * 16, 1 - core].astype(F32), axis=0)


def sum_call(sel, parts):
    vmem = pl.BlockSpec(memory_space=pltpu.VMEM)
    out = jax.ShapeDtypeStruct((4, 16, WCOLS), F32)
    return pl.pallas_call(
        sum_kernel,
        in_specs=[pl.BlockSpec(memory_space=pltpu.SMEM), vmem],
        out_specs=[vmem] * 2,
        out_shape=[out, out],
        compiler_params=params(),
        cost_estimate=cost(0.1),
        name="weight_sum",
    )(sel, parts)


def finish_kernel(sel_ref, own, got, w_ref, gain_ref, grad_ref, gain_grad_ref):
    first = sel_ref[0] == 0
    for core in range(2):
        for x in range(4):
            value = jnp.where(first == (core == 0), own[x], got[x])
            at = core * 1024 + x * 256
            grad_ref[:, at : at + 256] = value[:, :256]
            at = 2048 + (x // 2) * 512 + core * 256 + (x % 2) * HEAD
            grad_ref[:, at : at + HEAD] = value[:, 256:]
    total = jnp.sum(w_ref[...].astype(F32) * grad_ref[...], axis=1, keepdims=True)
    gain_grad_ref[...] = jnp.broadcast_to(total, (16, HEAD)).T[:1] / gain_ref[...]


def finish_call(sel, own, got, w_rows, gain_rows):
    vmem = pl.BlockSpec(memory_space=pltpu.VMEM)
    return pl.pallas_call(
        finish_kernel,
        in_specs=[pl.BlockSpec(memory_space=pltpu.SMEM)] + [vmem] * 4,
        out_specs=[vmem] * 2,
        out_shape=[jax.ShapeDtypeStruct((16, 3072), F32), jax.ShapeDtypeStruct((1, 16), F32)],
        compiler_params=params(),
        cost_estimate=cost(0.1),
        name="finish",
    )(sel, own, got, w_rows, gain_rows)


def inputs_kernel(sel_ref, x_ref, gain_ref, keep_ref, near_ref, far_ref, out_ref):
    x = x_ref[...].astype(F32)
    inv = lax.rsqrt(jnp.mean(x * x, axis=1, keepdims=True) + EPS)
    unit = x * inv
    here = keep_ref[...].astype(F32) + near_ref[...].astype(F32)
    d_normed = jnp.where(sel_ref[1] == 0, here, far_ref[...].astype(F32))
    scaled = d_normed * gain_ref[...]
    mean = jnp.mean(scaled * unit, axis=1, keepdims=True)
    out_ref[...] = (inv * (scaled - unit * mean)).astype(BF16)


def inputs_call(sel, x, gain, keep, near, far):
    tile = 128
    rows = pl.BlockSpec((tile, D), lambda t, sel: (t, 0))
    return pl.pallas_call(
        inputs_kernel,
        grid_spec=pltpu.PrefetchScalarGridSpec(
            num_scalar_prefetch=1,
            grid=(TOK // tile,),
            in_specs=[rows, pl.BlockSpec((1, D), lambda t, sel: (0, 0)), rows, rows, rows],
            out_specs=rows,
        ),
        out_shape=jax.ShapeDtypeStruct((TOK, D), BF16),
        compiler_params=params(),
        cost_estimate=cost(0.1),
        name="inputs_grad",
    )(sel, x, gain, keep, near, far)


def shift(value, axis, by):
    return lax.ppermute(value, axis, [(i, (i + by) % 4) for i in range(4)])


def swap_cores(value):
    return lax.ppermute(value, "c", [(0, 1), (1, 0)])


def after(value, *others):
    return lax.optimization_barrier((value,) + others)[0]


def body(inputs, gain, w, doc_lengths, out_grad):
    c, zl, y, x_at, zh = (lax.axis_index(a).astype(jnp.int32) for a in ("c", "zl", "y", "x", "zh"))
    resident = c == zl
    role = jnp.where(resident, 0, 1).astype(jnp.int32)
    sel = jnp.stack([c, role])
    x = inputs.reshape(TOK, D)
    grads = out_grad.reshape(TOK, 2048)
    gain2 = gain.reshape(1, D)
    near, far = 2 * y + zl, 2 * y + 1 - zl
    table = jnp.asarray(TABLE)

    g_mine = lax.dynamic_slice_in_dim(grads, zl * 1024, 1024, 1)
    g_other = lax.dynamic_slice_in_dim(grads, (1 - zl) * 1024, 1024, 1)
    g1 = lax.ppermute(g_other, PAIR, SPREAD1)
    g2 = lax.ppermute(g_mine, PAIR, SPREAD2)
    lengths = doc_lengths.reshape(16)

    normed, kv_mine, kv_other = kv_call(jnp.stack([zl, near, 15 - near]), x, gain2, w, table)

    r1 = lax.ppermute(kv_other, PAIR, SPREAD1)
    r2 = lax.ppermute(kv_mine, PAIR, SPREAD2)
    kv = jnp.stack([jnp.where(resident, kv_mine, r1), jnp.where(resident, r1, r2)])
    kv, g1, g2 = lax.optimization_barrier((kv, g1, g2))
    kv_from = {(4 - by) % 4: shift(kv, "y", by) for by in (2, 1, 3)}

    n1 = lax.ppermute(after(normed, r1, r2), PAIR, HOME_TO_VISITOR)
    sent = after(normed, r1, r2)
    n2 = lax.ppermute(sent, PAIR, SPREAD2)
    n3 = lax.ppermute(sent, PAIR, VISITOR_ACROSS)
    n_s, n_m = jnp.where(resident, normed, n1), jnp.where(resident, n3, n2)

    q = (
        q_call(jnp.stack([c, near, 15 - near]), n_s, w, table),
        q_call(jnp.stack([c, far, 15 - far]), n_m, w, table),
    )

    mine = after(jnp.where(resident, normed, n2), kv_from[1], kv_from[2], kv_from[3], *q)
    direct = {(4 - by) % 4: shift(mine, "x", by) for by in (2, 1, 3)}
    direct = [direct[r] for r in (1, 2, 3)]

    do = (jnp.where(resident, g_mine, g1), jnp.where(resident, g1, g2))

    lengths_near = lax.ppermute(after(lengths, n2), PAIR, HOME_TO_VISITOR)
    lengths = jnp.where(resident, lengths, lengths_near)
    upto = jnp.arange(16)
    ends = jnp.sum(jnp.where(upto[None, :] <= upto[:, None], lengths[None, :], 0), axis=1)
    blocks = []
    for r in range(CHIPS):
        a, b = 2 * ((y + r) % 4) + zl, 2 * ((y + r) % 4) + 1 - zl
        blocks += [a, 15 - a, b, 15 - b]
    own = jnp.stack(blocks[:4])
    positions = (own[:, None] * BLK + jnp.arange(BLK, dtype=jnp.int32)[None, :]).reshape(CHIP)
    start = jnp.max(jnp.where(positions[:, None] >= ends[None, :], ends[None, :], 0), axis=1).astype(jnp.int32)
    start = start.reshape(4, 1, BLK)
    lowest = start[:, 0, 0] // PAIR_TOK
    where = jnp.stack(
        blocks[:4]
        + [jnp.minimum(lowest[0], lowest[2]), jnp.minimum(lowest[1], lowest[3]), x_at, role]
        + blocks
    ).astype(jnp.int32)
    own_table = jnp.concatenate([lax.dynamic_slice_in_dim(table, b * BLK, BLK, 0) for b in blocks[:4]], axis=0)

    o_keep, o_give, dq, dq_to, dkv_to = attention_call(
        where, q, do, own_table, start, [kv, kv_from[1], kv_from[2], kv_from[3]]
    )

    others = [shift(dkv_to[by], "y", by) for by in (2, 1, 3)]
    jq = {(4 - by) % 4: shift(after(dq_to[by], *direct), "x", by) for by in (2, 1, 3)}
    jq = [dq_to[0], jq[1], jq[2], jq[3]]
    dn_q = dnorm_q_call(sel, dq, w)
    via = [swap_cores(after(piece, dn_q, *others, *jq[1:])) for piece in direct]
    joined_kv, jkv_to = joined_call(x_at.reshape(1), after(dkv_to[0], dn_q), others, own_table)
    jkv = {(4 - by) % 4: shift(after(jkv_to[by], *via), "x", by) for by in (2, 1, 3)}
    jkv = [jkv_to[0], jkv[1], jkv[2], jkv[3]]

    parts = weight_call(sel, (n_s, n_m), direct, via, jq, jkv)
    dn_keep, dn_give = dnorm_call(sel, after(dn_q, parts), joined_kv, w)
    parts = lax.all_to_all(parts.reshape(64, 2, 16, WCOLS), ("x", "zh", "y", "zl"), 0, 0, tiled=True)

    d1 = swap_cores(dn_give)
    summed = (dn_keep.astype(F32) + d1.astype(F32)).astype(BF16)
    d2 = lax.ppermute(summed, PAIR, SPREAD2)
    inputs_grad = inputs_call(sel, x, gain2, dn_keep, d1, d2)

    h1 = lax.ppermute(o_give, PAIR, RETURN1)
    h2 = lax.ppermute(o_keep, PAIR, SPREAD2)
    half_mine = jnp.where(resident, o_keep, h2)
    attended = jnp.concatenate(
        [jnp.where(zl == 0, half_mine, h1), jnp.where(zl == 0, h1, half_mine)], axis=1
    )

    keep, give = sum_call(sel, parts)
    got = swap_cores(give)
    at = ((((x_at * 2 + zh) * 2 + c) * 4 + y) * 2 + zl) * 16
    w_rows = lax.dynamic_slice_in_dim(w, at, 16, 0)
    gain_rows = lax.dynamic_slice_in_dim(gain2, at, 16, 1)
    qkv_grad, gain_grad = finish_call(sel, keep, got, w_rows, gain_rows)
    return (
        attended.reshape(1, 2, 1, BLK, 2048),
        inputs_grad.reshape(1, 2, 1, BLK, D),
        qkv_grad,
        gain_grad.reshape(16),
    )


def solution(mesh):
    fine = Mesh(mesh.devices.reshape(4, 2, 2, 4, 2), ("x", "zh", "c", "y", "zl"))
    dp, ctx = ("x", "zh", "c"), ("y", "zl")
    rows = P(dp, None, ctx, None, None)
    return jax.shard_map(
        body,
        mesh=fine,
        in_specs=(rows, P(), P(), P(dp, None), rows),
        out_specs=(rows, rows, P(dp + ctx, None), P(dp + ctx)),
        check_vma=False,
    )
```

```python
import jax
import jax.numpy as jnp
import numpy as np
from jax import lax
from jax.experimental import pallas as pl
from jax.experimental.pallas import tpu as pltpu
from jax.sharding import Mesh
from jax.sharding import PartitionSpec as P

HEAD = 128
GROUP = 4
D = 2048
BLK = 128
TOK = 256
CHIP = 512
NBLK = 16
WCOLS = 384
CHIPS = 4
PAIR_TOK = 2 * BLK
COLS = 4 * PAIR_TOK
WINDOW = 5
EPS = 1e-05
ROPE_BASE = 500000.0
SCALE = HEAD ** (-0.5)
EXP2_SCALE = SCALE * 1.4426950408889634
F32, BF16 = jnp.float32, jnp.bfloat16
VMEM_LIMIT = 56 * 1024 * 1024

ANGLES = np.arange(2048)[:, None] * ROPE_BASE ** (-2.0 * np.arange(64) / HEAD)
TABLE = np.concatenate([np.cos(ANGLES)] * 2 + [-np.sin(ANGLES), np.sin(ANGLES)], axis=1).astype(np.float32)

SPREAD1 = [(0, 2), (3, 1), (1, 0), (2, 3)]
SPREAD2 = [(1, 2), (2, 1)]
RETURN1 = [(2, 0), (1, 3), (0, 1), (3, 2)]
HOME_TO_VISITOR = [(0, 2), (3, 1)]
VISITOR_ACROSS = [(1, 0), (2, 3)]
PAIR = ("c", "zl")


def cost(us):
    return pl.CostEstimate(flops=int(us * 10**6), bytes_accessed=int(us * (1 << 20)), transcendentals=0)


def params():
    return pltpu.CompilerParams(vmem_limit_bytes=VMEM_LIMIT)


def dot_nt(a, b):
    return lax.dot_general(a, b, (((1,), (1,)), ((), ())), preferred_element_type=F32)


def dot_tn(a, b):
    return lax.dot_general(a, b, (((0,), (0,)), ((), ())), preferred_element_type=F32)


def dot_nn(a, b):
    return lax.dot_general(a, b, (((1,), (0,)), ((), ())), preferred_element_type=F32)


def rotate(v, cos, sin):
    return v * cos + pltpu.roll(v, 64, 1) * sin


def kv_kernel(sel_ref, x_ref, gain_ref, wk_ref, wv_ref, ta_ref, tb_ref, normed_ref, mine_ref, other_ref):
    step = pl.program_id(0)

    @pl.when(step == 0)
    def _():
        x = x_ref[...].astype(F32)
        inv = lax.rsqrt(jnp.mean(x * x, axis=1, keepdims=True) + EPS)
        normed_ref[...] = ((x * inv) * gain_ref[...]).astype(BF16)

    keys = dot_nn(normed_ref[...], wk_ref[...])
    values = dot_nn(normed_ref[...], wv_ref[...]).astype(BF16)
    table = jnp.concatenate([ta_ref[...], tb_ref[...]], axis=0)
    cos, sin = table[:, :HEAD], table[:, HEAD:]
    keys = jnp.concatenate(
        [rotate(keys[:, i * HEAD : (i + 1) * HEAD], cos, sin).astype(BF16) for i in range(2)], axis=1
    )

    @pl.when(step == 0)
    def _():
        mine_ref[:, :256] = keys
        mine_ref[:, 256:] = values

    @pl.when(step == 1)
    def _():
        other_ref[:, :256] = keys
        other_ref[:, 256:] = values


def kv_call(sel, x, gain, w, table):
    half = jax.ShapeDtypeStruct((TOK, 512), BF16)
    return pl.pallas_call(
        kv_kernel,
        grid_spec=pltpu.PrefetchScalarGridSpec(
            num_scalar_prefetch=1,
            grid=(2,),
            in_specs=[
                pl.BlockSpec((TOK, D), lambda t, sel: (0, 0)),
                pl.BlockSpec((1, D), lambda t, sel: (0, 0)),
                pl.BlockSpec((D, 256), lambda t, sel: (0, 8 + (sel[0] + t) % 2)),
                pl.BlockSpec((D, 256), lambda t, sel: (0, 10 + (sel[0] + t) % 2)),
                pl.BlockSpec((BLK, 256), lambda t, sel: (sel[1], 0)),
                pl.BlockSpec((BLK, 256), lambda t, sel: (sel[2], 0)),
            ],
            out_specs=[
                pl.BlockSpec((TOK, D), lambda t, sel: (0, 0)),
                pl.BlockSpec((TOK, 512), lambda t, sel: (0, 0)),
                pl.BlockSpec((TOK, 512), lambda t, sel: (0, 0)),
            ],
        ),
        out_shape=[jax.ShapeDtypeStruct((TOK, D), BF16), half, half],
        compiler_params=params(),
        cost_estimate=cost(0.01),
        name="kv_home",
    )(sel, x, gain, w, w, table, table)


def q_kernel(sel_ref, n_ref, w_ref, ta_ref, tb_ref, q_ref):
    out = dot_nn(n_ref[...], w_ref[...])
    table = jnp.concatenate([ta_ref[...], tb_ref[...]], axis=0)
    for i in range(4):
        cols = slice(i * HEAD, (i + 1) * HEAD)
        q_ref[:, cols] = rotate(out[:, cols], table[:, :HEAD], table[:, HEAD:]).astype(BF16)


def q_call(sel, normed, w, table):
    return pl.pallas_call(
        q_kernel,
        grid_spec=pltpu.PrefetchScalarGridSpec(
            num_scalar_prefetch=1,
            grid=(2,),
            in_specs=[
                pl.BlockSpec((TOK, D), lambda t, sel: (0, 0)),
                pl.BlockSpec((D, 512), lambda t, sel: (0, sel[0] * 2 + t)),
                pl.BlockSpec((BLK, 256), lambda t, sel: (sel[1], 0)),
                pl.BlockSpec((BLK, 256), lambda t, sel: (sel[2], 0)),
            ],
            out_specs=pl.BlockSpec((TOK, 512), lambda t, sel: (0, t)),
        ),
        out_shape=jax.ShapeDtypeStruct((TOK, 1024), BF16),
        compiler_params=params(),
        cost_estimate=cost(0.1),
        name="q_proj",
    )(sel, normed, w, table, table)


def attention_kernel(
    where_ref, qs_ref, qm_ref, dos_ref, dom_ref, table_ref, start_ref, kv_ref,
    keep_ref, give_ref, dq_ref, x0, x1, x2, x3, dkv_ref, kvbuf, acc, score, quarters,
):
    home = where_ref[7] == 0
    for r in range(CHIPS):
        for part in range(2):
            for half in range(2):
                block = where_ref[8 + r * 4 + part * 2 + half]
                kvbuf[block] = kv_ref[r, part, half * BLK : (half + 1) * BLK, :]
    acc[...] = jnp.zeros_like(acc)
    row = lax.broadcasted_iota(jnp.int32, (PAIR_TOK, COLS), 0)
    for p in range(2):
        rows = slice(p * BLK, (p + 1) * BLK)
        heads = [[slice((h * GROUP + g) * HEAD, (h * GROUP + g + 1) * HEAD) for g in range(GROUP)] for h in range(2)]
        kc = [slice(h * HEAD, (h + 1) * HEAD) for h in range(2)]
        vc = [slice(256 + h * HEAD, 256 + (h + 1) * HEAD) for h in range(2)]
        queries = [jnp.concatenate([ref[rows, g] for ref in (qs_ref, qm_ref) for g in heads[h]], axis=0) for h in range(2)]
        grads = [jnp.concatenate([ref[rows, g] for ref in (dos_ref, dom_ref) for g in heads[h]], axis=0) for h in range(2)]
        first = where_ref[4 + p]
        count = where_ref[p] // 2 - first + 1
        start = jnp.concatenate([start_ref[p]] * GROUP + [start_ref[2 + p]] * GROUP, axis=1)
        token = lax.broadcasted_iota(jnp.int32, (1, GROUP * BLK), 1) % BLK
        pos = jnp.concatenate([where_ref[p] * BLK + token, where_ref[2 + p] * BLK + token], axis=1)

        def pair(i, cols):
            return jnp.concatenate([kvbuf[2 * i, :, cols], kvbuf[2 * i + 1, :, cols]], axis=0)

        def score_step(i, tops, first=first, kc=kc, queries=queries, start=start, pos=pos):
            at = (first + i) * PAIR_TOK + row
            allowed = (at >= start) & (at <= pos)
            out = []
            for h in range(2):
                s = dot_nt(pair(first + i, kc[h]), queries[h])
                s = jnp.where(allowed, s, -jnp.inf)
                score[h, i] = s
                out.append(jnp.maximum(tops[h], jnp.max(s.reshape(PAIR_TOK // 8, 8, COLS), axis=0)))
            return tuple(out)

        tops = lax.fori_loop(0, count, score_step, (jnp.full((8, COLS), -jnp.inf, F32),) * 2)
        tops = [jnp.max(t, axis=0, keepdims=True) * EXP2_SCALE for t in tops]

        def value_step(i, carry, first=first, vc=vc, tops=tops):
            res = []
            for h in range(2):
                total, out = carry[h]
                e = jnp.exp2(score[h, i] * EXP2_SCALE - tops[h])
                score[h, i] = e
                total = total + jnp.sum(e.reshape(PAIR_TOK // 8, 8, COLS), axis=0)
                out = out + dot_tn(pair(first + i, vc[h]), e.astype(BF16))
                res.append((total, out))
            return tuple(res)

        carry = lax.fori_loop(
            0, count, value_step, ((jnp.zeros((8, COLS), F32), jnp.zeros((HEAD, COLS), F32)),) * 2
        )
        invs, deltas = [], []
        for h in range(2):
            total, out = carry[h]
            inv = 1.0 / jnp.sum(total, axis=0, keepdims=True)
            out = (out * inv).astype(BF16).astype(F32)
            deltas.append(jnp.sum(out * grads[h].astype(F32).T, axis=0, keepdims=True))
            invs.append(inv)
            for g in range(GROUP):
                of_s = out[:, g * BLK : (g + 1) * BLK].T.astype(BF16)
                of_m = out[:, (GROUP + g) * BLK : (GROUP + g + 1) * BLK].T.astype(BF16)
                keep_ref[rows, heads[h][g]] = jnp.where(home, of_s, of_m)
                give_ref[rows, heads[h][g]] = jnp.where(home, of_m, of_s)

        def grad_step(i, dqs, first=first, kc=kc, vc=vc, invs=invs, deltas=deltas, queries=queries, grads=grads):
            res = []
            j = first + i
            for h in range(2):
                keys, values = pair(j, kc[h]), pair(j, vc[h])
                prob = score[h, i] * invs[h]
                dp = dot_nt(values, grads[h])
                ds = (prob * (dp - deltas[h])).astype(BF16)
                dv = dot_nn(prob.astype(BF16), grads[h])
                dk = dot_nn(ds, queries[h])
                for k in range(2):
                    acc[2 * j + k, :, vc[h]] += dv[k * BLK : (k + 1) * BLK]
                    acc[2 * j + k, :, kc[h]] += dk[k * BLK : (k + 1) * BLK]
                res.append(dqs[h] + dot_tn(keys, ds))
            return tuple(res)

        dqs = lax.fori_loop(0, count, grad_step, (jnp.zeros((HEAD, COLS), F32),) * 2)
        for k in range(2):
            at = (2 * k + p) * BLK
            rows = slice(at, at + BLK)
            cos, sin = table_ref[rows, :HEAD] * SCALE, table_ref[rows, HEAD:] * SCALE
            for h in range(2):
                for g in range(GROUP):
                    at = (k * GROUP + g) * BLK
                    part = rotate(dqs[h][:, at : at + BLK].T, cos, -sin).astype(BF16)
                    dq_ref[rows, heads[h][g]] = part
                    j = h * GROUP + g
                    quarters[j // 2, rows, (j % 2) * HEAD : (j % 2 + 1) * HEAD] = part
    for r, out in enumerate((x0, x1, x2, x3)):
        out[...] = quarters[(where_ref[6] + r) % 4]
    for r in range(CHIPS):
        for j in range(4):
            at, rows = where_ref[8 + r * 4 + j], slice(j * BLK, (j + 1) * BLK)
            dkv_ref[r, rows, :256] = (acc[at, :, :256] * SCALE).astype(BF16)
            dkv_ref[r, rows, 256:] = acc[at, :, 256:].astype(BF16)


def attention_call(where, q, do, table, start, kv):
    vmem = pl.BlockSpec(memory_space=pltpu.VMEM)
    half = jax.ShapeDtypeStruct((TOK, 1024), BF16)
    out = pl.pallas_call(
        attention_kernel,
        in_specs=[pl.BlockSpec(memory_space=pltpu.SMEM)] + [vmem] * 7,
        out_specs=[vmem] * 8,
        out_shape=[half, half, jax.ShapeDtypeStruct((CHIP, 1024), BF16)]
        + [jax.ShapeDtypeStruct((CHIP, 256), BF16)] * 4
        + [jax.ShapeDtypeStruct((CHIPS, CHIP, 512), BF16)],
        scratch_shapes=[
            pltpu.VMEM((NBLK, BLK, 512), BF16),
            pltpu.VMEM((NBLK, BLK, 512), F32),
            pltpu.VMEM((2, WINDOW, PAIR_TOK, COLS), F32),
            pltpu.VMEM((4, CHIP, 256), BF16),
        ],
        compiler_params=params(),
        cost_estimate=cost(0.1),
        name="attention",
    )(where, *q, *do, table, start, kv)
    return out[0], out[1], out[2], out[3:7], out[7]


def joined_kernel(x_ref, parts_ref, table_ref, out_ref, j0, j1, j2, j3):
    total = jnp.sum(parts_ref[...].astype(F32), axis=0)
    for i in range(2):
        cols = slice(i * HEAD, (i + 1) * HEAD)
        out_ref[:, cols] = rotate(total[:, cols], table_ref[:, :HEAD], -table_ref[:, HEAD:]).astype(BF16)
    out_ref[:, 256:] = total[:, 256:].astype(BF16)
    for r, out in enumerate((j0, j1, j2, j3)):
        out[...] = out_ref[:, pl.ds(pl.multiple_of((x_ref[0] + r) % 4 * HEAD, HEAD), HEAD)]


def joined_call(x_at, parts, table):
    vmem = pl.BlockSpec(memory_space=pltpu.VMEM)
    out = pl.pallas_call(
        joined_kernel,
        in_specs=[pl.BlockSpec(memory_space=pltpu.SMEM)] + [vmem] * 2,
        out_specs=[vmem] * 5,
        out_shape=[jax.ShapeDtypeStruct((CHIP, 512), BF16)] + [jax.ShapeDtypeStruct((CHIP, HEAD), BF16)] * 4,
        compiler_params=params(),
        cost_estimate=cost(0.1),
        name="joined_kv",
    )(x_at, parts, table)
    return out[0], out[1:]


def dnorm_q_kernel(sel_ref, j_ref, w_ref, out_ref):
    out_ref[...] = dot_nt(j_ref[...], w_ref[...]).astype(BF16)


def dnorm_q_call(sel, jq, w):
    tile = 512
    return pl.pallas_call(
        dnorm_q_kernel,
        grid_spec=pltpu.PrefetchScalarGridSpec(
            num_scalar_prefetch=1,
            grid=(D // tile,),
            in_specs=[
                pl.BlockSpec((CHIP, 1024), lambda t, sel: (0, 0)),
                pl.BlockSpec((tile, 1024), lambda t, sel: (t, sel[0])),
            ],
            out_specs=pl.BlockSpec((CHIP, tile), lambda t, sel: (0, t)),
        ),
        out_shape=jax.ShapeDtypeStruct((CHIP, D), BF16),
        compiler_params=params(),
        cost_estimate=cost(0.01),
        name="d_normed_q",
    )(sel, jq, w)


def dnorm_kernel(sel_ref, part_ref, jkv_ref, wk_ref, wv_ref, keep_ref, give_ref):
    out = part_ref[...].astype(F32)
    out += dot_nt(jkv_ref[:, :256], wk_ref[...])
    out += dot_nt(jkv_ref[:, 256:], wv_ref[...])
    home = sel_ref[1] == 0
    of_s, of_m = out[:TOK].astype(BF16), out[TOK:].astype(BF16)
    keep_ref[...] = jnp.where(home, of_s, of_m)
    give_ref[...] = jnp.where(home, of_m, of_s)


def dnorm_call(sel, part, jkv, w):
    tile = 1024
    return pl.pallas_call(
        dnorm_kernel,
        grid_spec=pltpu.PrefetchScalarGridSpec(
            num_scalar_prefetch=1,
            grid=(D // tile,),
            in_specs=[
                pl.BlockSpec((CHIP, tile), lambda t, sel: (0, t)),
                pl.BlockSpec((CHIP, 512), lambda t, sel: (0, 0)),
                pl.BlockSpec((tile, 256), lambda t, sel: (t, 8 + sel[0])),
                pl.BlockSpec((tile, 256), lambda t, sel: (t, 10 + sel[0])),
            ],
            out_specs=[pl.BlockSpec((TOK, tile), lambda t, sel: (0, t))] * 2,
        ),
        out_shape=[jax.ShapeDtypeStruct((TOK, D), BF16)] * 2,
        compiler_params=params(),
        cost_estimate=cost(0.01),
        name="d_normed",
    )(sel, part, jkv, w, w)


def weight_kernel(sel_ref, ns, nm, d1, d2, d3, v1, v2, v3, q0, q1, q2, q3, k0, k1, k2, k3, out_ref, jt):
    role = sel_ref[1]
    pieces = ((ns, q0, k0, 0), (nm, q0, k0, TOK))
    for direct, via, q, k in ((d1, v1, q1, k1), (d2, v2, q2, k2), (d3, v3, q3, k3)):
        pieces += ((direct, q, k, role * TOK), (via, q, k, (1 - role) * TOK))

    @pl.when(pl.program_id(0) == 0)
    def _():
        for i, (_, q, k, at) in enumerate(pieces):
            jt[:256, i * TOK : (i + 1) * TOK] = q[pl.ds(at, TOK), :].T
            jt[256:, i * TOK : (i + 1) * TOK] = k[pl.ds(at, TOK), :].T

    out = jnp.zeros((WCOLS, out_ref.shape[0] * TOK), F32)
    for i, (n, _, _, _) in enumerate(pieces):
        out += dot_nn(jt[:, i * TOK : (i + 1) * TOK], n[...])
    for t in range(out_ref.shape[0]):
        part = out[:, t * TOK : (t + 1) * TOK].T.astype(BF16)
        for i in range(2):
            for k in range(8):
                at = i * 128 + k * 16
                out_ref[t, k, i] = part[at : at + 16]


def weight_call(sel, tokens, direct, via, jq, jkv):
    tile = 512
    part = pl.BlockSpec((TOK, tile), lambda t, sel: (0, t))
    return pl.pallas_call(
        weight_kernel,
        grid_spec=pltpu.PrefetchScalarGridSpec(
            num_scalar_prefetch=1,
            grid=(D // tile,),
            in_specs=[part] * 8
            + [pl.BlockSpec((CHIP, 256), lambda t, sel: (0, 0))] * 4
            + [pl.BlockSpec((CHIP, HEAD), lambda t, sel: (0, 0))] * 4,
            out_specs=pl.BlockSpec((tile // TOK, 8, 2, 16, WCOLS), lambda t, sel: (t, 0, 0, 0, 0)),
            scratch_shapes=[pltpu.VMEM((WCOLS, 8 * TOK), BF16)],
        ),
        out_shape=jax.ShapeDtypeStruct((8, 8, 2, 16, WCOLS), BF16),
        compiler_params=params(),
        cost_estimate=cost(0.1),
        name="weight_grad",
    )(sel, *tokens, *direct, *via, *jq, *jkv)


def sum_kernel(sel_ref, parts_ref, keep_ref, give_ref):
    core = sel_ref[0]
    for x in range(4):
        keep_ref[x] = jnp.sum(parts_ref[x * 16 : (x + 1) * 16, core].astype(F32), axis=0)
        give_ref[x] = jnp.sum(parts_ref[x * 16 : (x + 1) * 16, 1 - core].astype(F32), axis=0)


def sum_call(sel, parts):
    vmem = pl.BlockSpec(memory_space=pltpu.VMEM)
    out = jax.ShapeDtypeStruct((4, 16, WCOLS), F32)
    return pl.pallas_call(
        sum_kernel,
        in_specs=[pl.BlockSpec(memory_space=pltpu.SMEM), vmem],
        out_specs=[vmem] * 2,
        out_shape=[out, out],
        compiler_params=params(),
        cost_estimate=cost(0.1),
        name="weight_sum",
    )(sel, parts)


def finish_kernel(sel_ref, own, got, w_ref, gain_ref, grad_ref, gain_grad_ref):
    first = sel_ref[0] == 0
    for core in range(2):
        for x in range(4):
            value = jnp.where(first == (core == 0), own[x], got[x])
            at = core * 1024 + x * 256
            grad_ref[:, at : at + 256] = value[:, :256]
            at = 2048 + (x // 2) * 512 + core * 256 + (x % 2) * HEAD
            grad_ref[:, at : at + HEAD] = value[:, 256:]
    total = jnp.sum(w_ref[...].astype(F32) * grad_ref[...], axis=1, keepdims=True)
    gain_grad_ref[...] = jnp.broadcast_to(total, (16, HEAD)).T[:1] / gain_ref[...]


def finish_call(sel, own, got, w_rows, gain_rows):
    vmem = pl.BlockSpec(memory_space=pltpu.VMEM)
    return pl.pallas_call(
        finish_kernel,
        in_specs=[pl.BlockSpec(memory_space=pltpu.SMEM)] + [vmem] * 4,
        out_specs=[vmem] * 2,
        out_shape=[jax.ShapeDtypeStruct((16, 3072), F32), jax.ShapeDtypeStruct((1, 16), F32)],
        compiler_params=params(),
        cost_estimate=cost(0.1),
        name="finish",
    )(sel, own, got, w_rows, gain_rows)


def inputs_kernel(sel_ref, x_ref, gain_ref, keep_ref, near_ref, far_ref, out_ref):
    x = x_ref[...].astype(F32)
    inv = lax.rsqrt(jnp.mean(x * x, axis=1, keepdims=True) + EPS)
    unit = x * inv
    here = keep_ref[...].astype(F32) + near_ref[...].astype(F32)
    d_normed = jnp.where(sel_ref[1] == 0, here, far_ref[...].astype(F32))
    scaled = d_normed * gain_ref[...]
    mean = jnp.mean(scaled * unit, axis=1, keepdims=True)
    out_ref[...] = (inv * (scaled - unit * mean)).astype(BF16)


def inputs_call(sel, x, gain, keep, near, far):
    tile = 128
    rows = pl.BlockSpec((tile, D), lambda t, sel: (t, 0))
    return pl.pallas_call(
        inputs_kernel,
        grid_spec=pltpu.PrefetchScalarGridSpec(
            num_scalar_prefetch=1,
            grid=(TOK // tile,),
            in_specs=[rows, pl.BlockSpec((1, D), lambda t, sel: (0, 0)), rows, rows, rows],
            out_specs=rows,
        ),
        out_shape=jax.ShapeDtypeStruct((TOK, D), BF16),
        compiler_params=params(),
        cost_estimate=cost(0.1),
        name="inputs_grad",
    )(sel, x, gain, keep, near, far)


def shift(value, axis, by):
    return lax.ppermute(value, axis, [(i, (i + by) % 4) for i in range(4)])


def swap_cores(value):
    return lax.ppermute(value, "c", [(0, 1), (1, 0)])


def after(value, *others):
    return lax.optimization_barrier((value,) + others)[0]


def body(inputs, gain, w, doc_lengths, out_grad):
    c, zl, y, x_at, zh = (lax.axis_index(a).astype(jnp.int32) for a in ("c", "zl", "y", "x", "zh"))
    resident = c == zl
    role = jnp.where(resident, 0, 1).astype(jnp.int32)
    sel = jnp.stack([c, role])
    x = inputs.reshape(TOK, D)
    grads = out_grad.reshape(TOK, 2048)
    gain2 = gain.reshape(1, D)
    near, far = 2 * y + zl, 2 * y + 1 - zl
    table = jnp.asarray(TABLE)

    g_mine = lax.dynamic_slice_in_dim(grads, zl * 1024, 1024, 1)
    g_other = lax.dynamic_slice_in_dim(grads, (1 - zl) * 1024, 1024, 1)
    lengths = doc_lengths.reshape(16)
    lengths_near = lax.ppermute(lengths, PAIR, HOME_TO_VISITOR)

    normed, kv_mine, kv_other = kv_call(jnp.stack([zl, near, 15 - near]), x, gain2, w, table)

    r1 = lax.ppermute(after(kv_other, lengths_near), PAIR, SPREAD1)
    r2 = lax.ppermute(kv_mine, PAIR, SPREAD2)
    kv = jnp.stack([jnp.where(resident, kv_mine, r1), jnp.where(resident, r1, r2)])
    kv = jnp.broadcast_to(kv, (CHIPS,) + kv.shape)

    n1 = lax.ppermute(normed, PAIR, HOME_TO_VISITOR)
    sent = after(normed, kv, n1)
    kv_all = lax.all_to_all(after(kv, n1), "y", 0, 0, tiled=True)
    n2 = lax.ppermute(sent, PAIR, SPREAD2)
    n3 = lax.ppermute(sent, PAIR, VISITOR_ACROSS)
    n_s = jnp.where(resident, normed, n1)

    q_s = q_call(jnp.stack([c, near, 15 - near]), n_s, w, table)

    g1 = lax.ppermute(after(g_other, q_s), PAIR, SPREAD1)
    g2 = lax.ppermute(after(g_mine, q_s), PAIR, SPREAD2)
    g1, g2 = lax.optimization_barrier((g1, g2))
    do = (jnp.where(resident, g_mine, g1), jnp.where(resident, g1, g2))

    lengths = jnp.where(resident, lengths, lengths_near)
    upto = jnp.arange(16)
    ends = jnp.sum(jnp.where(upto[None, :] <= upto[:, None], lengths[None, :], 0), axis=1)
    own = [near, 15 - near, far, 15 - far]
    blocks = []
    for r in range(CHIPS):
        a, b = 2 * r + zl, 2 * r + 1 - zl
        blocks += [a, 15 - a, b, 15 - b]
    positions = (jnp.stack(own)[:, None] * BLK + jnp.arange(BLK, dtype=jnp.int32)[None, :]).reshape(CHIP)
    start = jnp.max(jnp.where(positions[:, None] >= ends[None, :], ends[None, :], 0), axis=1).astype(jnp.int32)
    start = start.reshape(4, 1, BLK)
    lowest = start[:, 0, 0] // PAIR_TOK
    where = jnp.stack(
        own
        + [jnp.minimum(lowest[0], lowest[2]), jnp.minimum(lowest[1], lowest[3]), x_at, role]
        + blocks
    ).astype(jnp.int32)
    own_table = jnp.concatenate([lax.dynamic_slice_in_dim(table, b * BLK, BLK, 0) for b in own], axis=0)

    n3 = after(n3, q_s, where, start, own_table)
    n_m = jnp.where(resident, n3, n2)
    q = (q_s, q_call(jnp.stack([c, far, 15 - far]), n_m, w, table))

    mine = after(jnp.where(resident, normed, n2), g1, g2)
    direct = {(4 - by) % 4: shift(mine, "x", by) for by in (2, 1, 3)}
    direct = [direct[r] for r in (1, 2, 3)]

    o_keep, o_give, dq, dq_to, dkv = attention_call(
        where, q, do, own_table, start, kv_all
    )

    dkv = lax.all_to_all(dkv, "y", 0, 0, tiled=True)
    dn_q = dnorm_q_call(sel, dq, w)
    jq = {(4 - by) % 4: shift(after(dq_to[by], *direct), "x", by) for by in (2, 1, 3)}
    jq = [dq_to[0], jq[1], jq[2], jq[3]]
    h1 = lax.ppermute(o_give, PAIR, RETURN1)
    h2 = lax.ppermute(o_keep, PAIR, SPREAD2)
    half_mine = jnp.where(resident, o_keep, h2)
    attended = jnp.concatenate(
        [jnp.where(zl == 0, half_mine, h1), jnp.where(zl == 0, h1, half_mine)], axis=1
    )

    via = [swap_cores(after(piece, dn_q, h2, *jq[1:])) for piece in direct]
    joined_kv, jkv_to = joined_call(x_at.reshape(1), after(dkv, dn_q, attended, *via), own_table)
    jkv = {(4 - by) % 4: shift(jkv_to[by], "x", by) for by in (2, 1, 3)}
    jkv = [jkv_to[0], jkv[1], jkv[2], jkv[3]]

    dn_keep, dn_give = dnorm_call(sel, dn_q, joined_kv, w)
    d1 = swap_cores(dn_give)
    summed = (dn_keep.astype(F32) + after(d1, *jkv).astype(F32)).astype(BF16)
    d2 = lax.ppermute(summed, PAIR, SPREAD2)
    parts = weight_call(after(sel, summed), (n_s, n_m), direct, via, jq, jkv)
    parts = lax.all_to_all(after(parts, d2).reshape(64, 2, 16, WCOLS), ("x", "zh", "y", "zl"), 0, 0, tiled=True)

    inputs_grad = inputs_call(sel, x, gain2, dn_keep, d1, d2)

    at = ((((x_at * 2 + zh) * 2 + c) * 4 + y) * 2 + zl) * 16
    w_rows = lax.dynamic_slice_in_dim(w, at, 16, 0)
    gain_rows = lax.dynamic_slice_in_dim(gain2, at, 16, 1)
    keep, give = sum_call(sel, after(parts, inputs_grad, w_rows, gain_rows))
    got = swap_cores(give)
    qkv_grad, gain_grad = finish_call(sel, keep, got, w_rows, gain_rows)
    return (
        attended.reshape(1, 2, 1, BLK, 2048),
        inputs_grad.reshape(1, 2, 1, BLK, D),
        qkv_grad,
        gain_grad.reshape(16),
    )


def solution(mesh):
    fine = Mesh(mesh.devices.reshape(4, 2, 2, 4, 2), ("x", "zh", "c", "y", "zl"))
    dp, ctx = ("x", "zh", "c"), ("y", "zl")
    rows = P(dp, None, ctx, None, None)
    return jax.shard_map(
        body,
        mesh=fine,
        in_specs=(rows, P(), P(), P(dp, None), rows),
        out_specs=(rows, rows, P(dp + ctx, None), P(dp + ctx)),
        check_vma=False,
    )
```

```python
import jax
import jax.numpy as jnp
import numpy as np
from jax import lax
from jax.experimental import pallas as pl
from jax.experimental.pallas import tpu as pltpu
from jax.sharding import Mesh
from jax.sharding import PartitionSpec as P

HEAD = 128
GROUP = 4
D = 2048
BLK = 128
TOK = 256
CHIP = 512
NBLK = 16
WCOLS = 384
CHIPS = 4
PAIR_TOK = 2 * BLK
COLS = 4 * PAIR_TOK
WINDOW = 5
EPS = 1e-05
ROPE_BASE = 500000.0
SCALE = HEAD ** (-0.5)
EXP2_SCALE = SCALE * 1.4426950408889634
F32, BF16 = jnp.float32, jnp.bfloat16
VMEM_LIMIT = 56 * 1024 * 1024

ANGLES = np.arange(2048)[:, None] * ROPE_BASE ** (-2.0 * np.arange(64) / HEAD)
TABLE = np.concatenate([np.cos(ANGLES)] * 2 + [-np.sin(ANGLES), np.sin(ANGLES)], axis=1).astype(np.float32)

SPREAD1 = [(0, 2), (3, 1), (1, 0), (2, 3)]
SPREAD2 = [(1, 2), (2, 1)]
RETURN1 = [(2, 0), (1, 3), (0, 1), (3, 2)]
HOME_TO_VISITOR = [(0, 2), (3, 1)]
VISITOR_ACROSS = [(1, 0), (2, 3)]
PAIR = ("c", "zl")


def cost(us):
    return pl.CostEstimate(flops=int(us * 10**6), bytes_accessed=int(us * (1 << 20)), transcendentals=0)


def params():
    return pltpu.CompilerParams(vmem_limit_bytes=VMEM_LIMIT)


def dot_nt(a, b):
    return lax.dot_general(a, b, (((1,), (1,)), ((), ())), preferred_element_type=F32)


def dot_tn(a, b):
    return lax.dot_general(a, b, (((0,), (0,)), ((), ())), preferred_element_type=F32)


def dot_nn(a, b):
    return lax.dot_general(a, b, (((1,), (0,)), ((), ())), preferred_element_type=F32)


def rotate(v, cos, sin):
    return v * cos + pltpu.roll(v, 64, 1) * sin


def kv_kernel(sel_ref, x_ref, gain_ref, wk_ref, wv_ref, ta_ref, tb_ref, normed_ref, mine_ref, other_ref):
    step = pl.program_id(0)

    @pl.when(step == 0)
    def _():
        x = x_ref[...].astype(F32)
        inv = lax.rsqrt(jnp.mean(x * x, axis=1, keepdims=True) + EPS)
        normed_ref[...] = ((x * inv) * gain_ref[...]).astype(BF16)

    keys = dot_nn(normed_ref[...], wk_ref[...])
    values = dot_nn(normed_ref[...], wv_ref[...]).astype(BF16)
    table = jnp.concatenate([ta_ref[...], tb_ref[...]], axis=0)
    cos, sin = table[:, :HEAD], table[:, HEAD:]
    keys = jnp.concatenate(
        [rotate(keys[:, i * HEAD : (i + 1) * HEAD], cos, sin).astype(BF16) for i in range(2)], axis=1
    )

    @pl.when(step == 0)
    def _():
        mine_ref[:, :256] = keys
        mine_ref[:, 256:] = values

    @pl.when(step == 1)
    def _():
        other_ref[:, :256] = keys
        other_ref[:, 256:] = values


def kv_call(sel, x, gain, w, table):
    half = jax.ShapeDtypeStruct((TOK, 512), BF16)
    return pl.pallas_call(
        kv_kernel,
        grid_spec=pltpu.PrefetchScalarGridSpec(
            num_scalar_prefetch=1,
            grid=(2,),
            in_specs=[
                pl.BlockSpec((TOK, D), lambda t, sel: (0, 0)),
                pl.BlockSpec((1, D), lambda t, sel: (0, 0)),
                pl.BlockSpec((D, 256), lambda t, sel: (0, 8 + (sel[0] + t) % 2)),
                pl.BlockSpec((D, 256), lambda t, sel: (0, 10 + (sel[0] + t) % 2)),
                pl.BlockSpec((BLK, 256), lambda t, sel: (sel[1], 0)),
                pl.BlockSpec((BLK, 256), lambda t, sel: (sel[2], 0)),
            ],
            out_specs=[
                pl.BlockSpec((TOK, D), lambda t, sel: (0, 0)),
                pl.BlockSpec((TOK, 512), lambda t, sel: (0, 0)),
                pl.BlockSpec((TOK, 512), lambda t, sel: (0, 0)),
            ],
        ),
        out_shape=[jax.ShapeDtypeStruct((TOK, D), BF16), half, half],
        compiler_params=params(),
        cost_estimate=cost(0.01),
        name="kv_home",
    )(sel, x, gain, w, w, table, table)


def q_kernel(sel_ref, n_ref, w_ref, ta_ref, tb_ref, q_ref):
    out = dot_nn(n_ref[...], w_ref[...])
    table = jnp.concatenate([ta_ref[...], tb_ref[...]], axis=0)
    for i in range(4):
        cols = slice(i * HEAD, (i + 1) * HEAD)
        q_ref[:, cols] = rotate(out[:, cols], table[:, :HEAD], table[:, HEAD:]).astype(BF16)


def q_call(sel, normed, w, table):
    return pl.pallas_call(
        q_kernel,
        grid_spec=pltpu.PrefetchScalarGridSpec(
            num_scalar_prefetch=1,
            grid=(2,),
            in_specs=[
                pl.BlockSpec((TOK, D), lambda t, sel: (0, 0)),
                pl.BlockSpec((D, 512), lambda t, sel: (0, sel[0] * 2 + t)),
                pl.BlockSpec((BLK, 256), lambda t, sel: (sel[1], 0)),
                pl.BlockSpec((BLK, 256), lambda t, sel: (sel[2], 0)),
            ],
            out_specs=pl.BlockSpec((TOK, 512), lambda t, sel: (0, t)),
        ),
        out_shape=jax.ShapeDtypeStruct((TOK, 1024), BF16),
        compiler_params=params(),
        cost_estimate=cost(0.1),
        name="q_proj",
    )(sel, normed, w, table, table)


def attention_kernel(
    where_ref, qs_ref, qm_ref, dos_ref, dom_ref, table_ref, start_ref, kv_ref,
    keep_ref, give_ref, dq_ref, x0, x1, x2, x3, dkv_ref, kvbuf, acc, score, quarters,
):
    home = where_ref[7] == 0
    for r in range(CHIPS):
        for part in range(2):
            for half in range(2):
                block = where_ref[8 + r * 4 + part * 2 + half]
                kvbuf[block] = kv_ref[r, part, half * BLK : (half + 1) * BLK, :]
    acc[...] = jnp.zeros_like(acc)
    row = lax.broadcasted_iota(jnp.int32, (PAIR_TOK, COLS), 0)
    for p in range(2):
        rows = slice(p * BLK, (p + 1) * BLK)
        heads = [[slice((h * GROUP + g) * HEAD, (h * GROUP + g + 1) * HEAD) for g in range(GROUP)] for h in range(2)]
        kc = [slice(h * HEAD, (h + 1) * HEAD) for h in range(2)]
        vc = [slice(256 + h * HEAD, 256 + (h + 1) * HEAD) for h in range(2)]
        queries = [jnp.concatenate([ref[rows, g] for ref in (qs_ref, qm_ref) for g in heads[h]], axis=0) for h in range(2)]
        grads = [jnp.concatenate([ref[rows, g] for ref in (dos_ref, dom_ref) for g in heads[h]], axis=0) for h in range(2)]
        first = where_ref[4 + p]
        count = where_ref[p] // 2 - first + 1
        start = jnp.concatenate([start_ref[p]] * GROUP + [start_ref[2 + p]] * GROUP, axis=1)
        token = lax.broadcasted_iota(jnp.int32, (1, GROUP * BLK), 1) % BLK
        pos = jnp.concatenate([where_ref[p] * BLK + token, where_ref[2 + p] * BLK + token], axis=1)

        def pair(i, cols):
            return jnp.concatenate([kvbuf[2 * i, :, cols], kvbuf[2 * i + 1, :, cols]], axis=0)

        def score_step(i, tops, first=first, kc=kc, queries=queries, start=start, pos=pos):
            at = (first + i) * PAIR_TOK + row
            allowed = (at >= start) & (at <= pos)
            out = []
            for h in range(2):
                s = dot_nt(pair(first + i, kc[h]), queries[h])
                s = jnp.where(allowed, s, -jnp.inf)
                score[h, i] = s
                out.append(jnp.maximum(tops[h], jnp.max(s.reshape(PAIR_TOK // 8, 8, COLS), axis=0)))
            return tuple(out)

        tops = lax.fori_loop(0, count, score_step, (jnp.full((8, COLS), -jnp.inf, F32),) * 2)
        tops = [jnp.max(t, axis=0, keepdims=True) * EXP2_SCALE for t in tops]

        def value_step(i, carry, first=first, vc=vc, tops=tops):
            res = []
            for h in range(2):
                total, out = carry[h]
                e = jnp.exp2(score[h, i] * EXP2_SCALE - tops[h])
                score[h, i] = e
                total = total + jnp.sum(e.reshape(PAIR_TOK // 8, 8, COLS), axis=0)
                out = out + dot_tn(pair(first + i, vc[h]), e.astype(BF16))
                res.append((total, out))
            return tuple(res)

        carry = lax.fori_loop(
            0, count, value_step, ((jnp.zeros((8, COLS), F32), jnp.zeros((HEAD, COLS), F32)),) * 2
        )
        invs, deltas = [], []
        for h in range(2):
            total, out = carry[h]
            inv = 1.0 / jnp.sum(total, axis=0, keepdims=True)
            out = (out * inv).astype(BF16).astype(F32)
            deltas.append(jnp.sum(out * grads[h].astype(F32).T, axis=0, keepdims=True))
            invs.append(inv)
            for g in range(GROUP):
                of_s = out[:, g * BLK : (g + 1) * BLK].T.astype(BF16)
                of_m = out[:, (GROUP + g) * BLK : (GROUP + g + 1) * BLK].T.astype(BF16)
                keep_ref[rows, heads[h][g]] = jnp.where(home, of_s, of_m)
                give_ref[rows, heads[h][g]] = jnp.where(home, of_m, of_s)

        def grad_step(i, dqs, first=first, kc=kc, vc=vc, invs=invs, deltas=deltas, queries=queries, grads=grads):
            res = []
            j = first + i
            for h in range(2):
                keys, values = pair(j, kc[h]), pair(j, vc[h])
                prob = score[h, i] * invs[h]
                dp = dot_nt(values, grads[h])
                ds = (prob * (dp - deltas[h])).astype(BF16)
                dv = dot_nn(prob.astype(BF16), grads[h])
                dk = dot_nn(ds, queries[h])
                for k in range(2):
                    acc[2 * j + k, :, vc[h]] += dv[k * BLK : (k + 1) * BLK]
                    acc[2 * j + k, :, kc[h]] += dk[k * BLK : (k + 1) * BLK]
                res.append(dqs[h] + dot_tn(keys, ds))
            return tuple(res)

        dqs = lax.fori_loop(0, count, grad_step, (jnp.zeros((HEAD, COLS), F32),) * 2)
        for k in range(2):
            at = (2 * k + p) * BLK
            rows = slice(at, at + BLK)
            cos, sin = table_ref[rows, :HEAD] * SCALE, table_ref[rows, HEAD:] * SCALE
            for h in range(2):
                for g in range(GROUP):
                    at = (k * GROUP + g) * BLK
                    part = rotate(dqs[h][:, at : at + BLK].T, cos, -sin).astype(BF16)
                    dq_ref[rows, heads[h][g]] = part
                    j = h * GROUP + g
                    quarters[j // 2, rows, (j % 2) * HEAD : (j % 2 + 1) * HEAD] = part
    for r, out in enumerate((x0, x1, x2, x3)):
        out[...] = quarters[(where_ref[6] + r) % 4]
    for r in range(CHIPS):
        for j in range(4):
            at, rows = where_ref[8 + r * 4 + j], slice(j * BLK, (j + 1) * BLK)
            dkv_ref[r, rows, :256] = (acc[at, :, :256] * SCALE).astype(BF16)
            dkv_ref[r, rows, 256:] = acc[at, :, 256:].astype(BF16)


def attention_call(where, q, do, table, start, kv):
    vmem = pl.BlockSpec(memory_space=pltpu.VMEM)
    half = jax.ShapeDtypeStruct((TOK, 1024), BF16)
    out = pl.pallas_call(
        attention_kernel,
        in_specs=[pl.BlockSpec(memory_space=pltpu.SMEM)] + [vmem] * 7,
        out_specs=[vmem] * 8,
        out_shape=[half, half, jax.ShapeDtypeStruct((CHIP, 1024), BF16)]
        + [jax.ShapeDtypeStruct((CHIP, 256), BF16)] * 4
        + [jax.ShapeDtypeStruct((CHIPS, CHIP, 512), BF16)],
        scratch_shapes=[
            pltpu.VMEM((NBLK, BLK, 512), BF16),
            pltpu.VMEM((NBLK, BLK, 512), F32),
            pltpu.VMEM((2, WINDOW, PAIR_TOK, COLS), F32),
            pltpu.VMEM((4, CHIP, 256), BF16),
        ],
        compiler_params=params(),
        cost_estimate=cost(0.1),
        name="attention",
    )(where, *q, *do, table, start, kv)
    return out[0], out[1], out[2], out[3:7], out[7]


def joined_kernel(x_ref, parts_ref, table_ref, out_ref, j0, j1, j2, j3):
    total = jnp.sum(parts_ref[...].astype(F32), axis=0)
    for i in range(2):
        cols = slice(i * HEAD, (i + 1) * HEAD)
        out_ref[:, cols] = rotate(total[:, cols], table_ref[:, :HEAD], -table_ref[:, HEAD:]).astype(BF16)
    out_ref[:, 256:] = total[:, 256:].astype(BF16)
    for r, out in enumerate((j0, j1, j2, j3)):
        out[...] = out_ref[:, pl.ds(pl.multiple_of((x_ref[0] + r) % 4 * HEAD, HEAD), HEAD)]


def joined_call(x_at, parts, table):
    vmem = pl.BlockSpec(memory_space=pltpu.VMEM)
    out = pl.pallas_call(
        joined_kernel,
        in_specs=[pl.BlockSpec(memory_space=pltpu.SMEM)] + [vmem] * 2,
        out_specs=[vmem] * 5,
        out_shape=[jax.ShapeDtypeStruct((CHIP, 512), BF16)] + [jax.ShapeDtypeStruct((CHIP, HEAD), BF16)] * 4,
        compiler_params=params(),
        cost_estimate=cost(0.1),
        name="joined_kv",
    )(x_at, parts, table)
    return out[0], out[1:]


def dnorm_q_kernel(sel_ref, j_ref, w_ref, out_ref):
    out_ref[...] = dot_nt(j_ref[...], w_ref[...]).astype(BF16)


def dnorm_q_call(sel, jq, w):
    tile = 512
    return pl.pallas_call(
        dnorm_q_kernel,
        grid_spec=pltpu.PrefetchScalarGridSpec(
            num_scalar_prefetch=1,
            grid=(D // tile,),
            in_specs=[
                pl.BlockSpec((CHIP, 1024), lambda t, sel: (0, 0)),
                pl.BlockSpec((tile, 1024), lambda t, sel: (t, sel[0])),
            ],
            out_specs=pl.BlockSpec((CHIP, tile), lambda t, sel: (0, t)),
        ),
        out_shape=jax.ShapeDtypeStruct((CHIP, D), BF16),
        compiler_params=params(),
        cost_estimate=cost(0.01),
        name="d_normed_q",
    )(sel, jq, w)


def dnorm_kernel(sel_ref, part_ref, jkv_ref, wk_ref, wv_ref, keep_ref, give_ref):
    out = part_ref[...].astype(F32)
    out += dot_nt(jkv_ref[:, :256], wk_ref[...])
    out += dot_nt(jkv_ref[:, 256:], wv_ref[...])
    home = sel_ref[1] == 0
    of_s, of_m = out[:TOK].astype(BF16), out[TOK:].astype(BF16)
    keep_ref[...] = jnp.where(home, of_s, of_m)
    give_ref[...] = jnp.where(home, of_m, of_s)


def dnorm_call(sel, part, jkv, w):
    tile = 1024
    return pl.pallas_call(
        dnorm_kernel,
        grid_spec=pltpu.PrefetchScalarGridSpec(
            num_scalar_prefetch=1,
            grid=(D // tile,),
            in_specs=[
                pl.BlockSpec((CHIP, tile), lambda t, sel: (0, t)),
                pl.BlockSpec((CHIP, 512), lambda t, sel: (0, 0)),
                pl.BlockSpec((tile, 256), lambda t, sel: (t, 8 + sel[0])),
                pl.BlockSpec((tile, 256), lambda t, sel: (t, 10 + sel[0])),
            ],
            out_specs=[pl.BlockSpec((TOK, tile), lambda t, sel: (0, t))] * 2,
        ),
        out_shape=[jax.ShapeDtypeStruct((TOK, D), BF16)] * 2,
        compiler_params=params(),
        cost_estimate=cost(0.01),
        name="d_normed",
    )(sel, part, jkv, w, w)


def weight_kernel(sel_ref, ns, nm, d1, d2, d3, v1, v2, v3, q0, q1, q2, q3, k0, k1, k2, k3, out_ref, jt):
    role = sel_ref[1]
    pieces = ((ns, q0, k0, 0), (nm, q0, k0, TOK))
    for direct, via, q, k in ((d1, v1, q1, k1), (d2, v2, q2, k2), (d3, v3, q3, k3)):
        pieces += ((direct, q, k, role * TOK), (via, q, k, (1 - role) * TOK))

    @pl.when(pl.program_id(0) == 0)
    def _():
        for i, (_, q, k, at) in enumerate(pieces):
            jt[:256, i * TOK : (i + 1) * TOK] = q[pl.ds(at, TOK), :].T
            jt[256:, i * TOK : (i + 1) * TOK] = k[pl.ds(at, TOK), :].T

    out = jnp.zeros((WCOLS, out_ref.shape[0] * TOK), F32)
    for i, (n, _, _, _) in enumerate(pieces):
        out += dot_nn(jt[:, i * TOK : (i + 1) * TOK], n[...])
    for t in range(out_ref.shape[0]):
        part = out[:, t * TOK : (t + 1) * TOK].T.astype(BF16)
        for i in range(2):
            for k in range(8):
                at = i * 128 + k * 16
                out_ref[t, k, i] = part[at : at + 16]


def weight_call(sel, tokens, direct, via, jq, jkv):
    tile = 512
    part = pl.BlockSpec((TOK, tile), lambda t, sel: (0, t))
    return pl.pallas_call(
        weight_kernel,
        grid_spec=pltpu.PrefetchScalarGridSpec(
            num_scalar_prefetch=1,
            grid=(D // tile,),
            in_specs=[part] * 8
            + [pl.BlockSpec((CHIP, 256), lambda t, sel: (0, 0))] * 4
            + [pl.BlockSpec((CHIP, HEAD), lambda t, sel: (0, 0))] * 4,
            out_specs=pl.BlockSpec((tile // TOK, 8, 2, 16, WCOLS), lambda t, sel: (t, 0, 0, 0, 0)),
            scratch_shapes=[pltpu.VMEM((WCOLS, 8 * TOK), BF16)],
        ),
        out_shape=jax.ShapeDtypeStruct((8, 8, 2, 16, WCOLS), BF16),
        compiler_params=params(),
        cost_estimate=cost(0.1),
        name="weight_grad",
    )(sel, *tokens, *direct, *via, *jq, *jkv)


def sum_kernel(sel_ref, parts_ref, keep_ref, give_ref):
    core = sel_ref[0]
    for x in range(4):
        keep_ref[x] = jnp.sum(parts_ref[x * 16 : (x + 1) * 16, core].astype(F32), axis=0)
        give_ref[x] = jnp.sum(parts_ref[x * 16 : (x + 1) * 16, 1 - core].astype(F32), axis=0)


def sum_call(sel, parts):
    vmem = pl.BlockSpec(memory_space=pltpu.VMEM)
    out = jax.ShapeDtypeStruct((4, 16, WCOLS), F32)
    return pl.pallas_call(
        sum_kernel,
        in_specs=[pl.BlockSpec(memory_space=pltpu.SMEM), vmem],
        out_specs=[vmem] * 2,
        out_shape=[out, out],
        compiler_params=params(),
        cost_estimate=cost(0.1),
        name="weight_sum",
    )(sel, parts)


def finish_kernel(sel_ref, own, got, w_ref, gain_ref, grad_ref, gain_grad_ref):
    first = sel_ref[0] == 0
    for core in range(2):
        for x in range(4):
            value = jnp.where(first == (core == 0), own[x], got[x])
            at = core * 1024 + x * 256
            grad_ref[:, at : at + 256] = value[:, :256]
            at = 2048 + (x // 2) * 512 + core * 256 + (x % 2) * HEAD
            grad_ref[:, at : at + HEAD] = value[:, 256:]
    total = jnp.sum(w_ref[...].astype(F32) * grad_ref[...], axis=1, keepdims=True)
    gain_grad_ref[...] = jnp.broadcast_to(total, (16, HEAD)).T[:1] / gain_ref[...]


def finish_call(sel, own, got, w_rows, gain_rows):
    vmem = pl.BlockSpec(memory_space=pltpu.VMEM)
    return pl.pallas_call(
        finish_kernel,
        in_specs=[pl.BlockSpec(memory_space=pltpu.SMEM)] + [vmem] * 4,
        out_specs=[vmem] * 2,
        out_shape=[jax.ShapeDtypeStruct((16, 3072), F32), jax.ShapeDtypeStruct((1, 16), F32)],
        compiler_params=params(),
        cost_estimate=cost(0.1),
        name="finish",
    )(sel, own, got, w_rows, gain_rows)


def inputs_kernel(sel_ref, x_ref, gain_ref, keep_ref, near_ref, far_ref, out_ref):
    x = x_ref[...].astype(F32)
    inv = lax.rsqrt(jnp.mean(x * x, axis=1, keepdims=True) + EPS)
    unit = x * inv
    here = keep_ref[...].astype(F32) + near_ref[...].astype(F32)
    d_normed = jnp.where(sel_ref[1] == 0, here, far_ref[...].astype(F32))
    scaled = d_normed * gain_ref[...]
    mean = jnp.mean(scaled * unit, axis=1, keepdims=True)
    out_ref[...] = (inv * (scaled - unit * mean)).astype(BF16)


def inputs_call(sel, x, gain, keep, near, far):
    tile = 128
    rows = pl.BlockSpec((tile, D), lambda t, sel: (t, 0))
    return pl.pallas_call(
        inputs_kernel,
        grid_spec=pltpu.PrefetchScalarGridSpec(
            num_scalar_prefetch=1,
            grid=(TOK // tile,),
            in_specs=[rows, pl.BlockSpec((1, D), lambda t, sel: (0, 0)), rows, rows, rows],
            out_specs=rows,
        ),
        out_shape=jax.ShapeDtypeStruct((TOK, D), BF16),
        compiler_params=params(),
        cost_estimate=cost(0.1),
        name="inputs_grad",
    )(sel, x, gain, keep, near, far)


def shift(value, axis, by):
    return lax.ppermute(value, axis, [(i, (i + by) % 4) for i in range(4)])


def swap_cores(value):
    return lax.ppermute(value, "c", [(0, 1), (1, 0)])


def after(value, *others):
    return lax.optimization_barrier((value,) + others)[0]


def body(inputs, gain, w, doc_lengths, out_grad):
    c, zl, y, x_at, zh = (lax.axis_index(a).astype(jnp.int32) for a in ("c", "zl", "y", "x", "zh"))
    resident = c == zl
    role = jnp.where(resident, 0, 1).astype(jnp.int32)
    sel = jnp.stack([c, role])
    x = inputs.reshape(TOK, D)
    grads = out_grad.reshape(TOK, 2048)
    gain2 = gain.reshape(1, D)
    near, far = 2 * y + zl, 2 * y + 1 - zl
    table = jnp.asarray(TABLE)

    g_mine = lax.dynamic_slice_in_dim(grads, zl * 1024, 1024, 1)
    g_other = lax.dynamic_slice_in_dim(grads, (1 - zl) * 1024, 1024, 1)
    lengths = doc_lengths.reshape(16)
    lengths_near = lax.ppermute(lengths, PAIR, HOME_TO_VISITOR)

    normed, kv_mine, kv_other = kv_call(jnp.stack([zl, near, 15 - near]), x, gain2, w, table)

    r1 = lax.ppermute(after(kv_other, lengths_near), PAIR, SPREAD1)
    r2 = lax.ppermute(kv_mine, PAIR, SPREAD2)
    kv = jnp.stack([jnp.where(resident, kv_mine, r1), jnp.where(resident, r1, r2)])
    kv = jnp.broadcast_to(kv, (CHIPS,) + kv.shape)

    n1 = lax.ppermute(normed, PAIR, HOME_TO_VISITOR)
    sent = after(normed, kv, n1)
    kv_all = lax.all_to_all(after(kv, n1), "y", 0, 0, tiled=True)
    n2 = lax.ppermute(sent, PAIR, SPREAD2)
    n3 = lax.ppermute(sent, PAIR, VISITOR_ACROSS)
    n_s = jnp.where(resident, normed, n1)

    q_s = q_call(jnp.stack([c, near, 15 - near]), n_s, w, table)

    g1 = lax.ppermute(after(g_other, q_s), PAIR, SPREAD1)
    g2 = lax.ppermute(after(g_mine, q_s), PAIR, SPREAD2)

    lengths = jnp.where(resident, lengths, lengths_near)
    upto = jnp.arange(16)
    ends = jnp.sum(jnp.where(upto[None, :] <= upto[:, None], lengths[None, :], 0), axis=1)
    own = [near, 15 - near, far, 15 - far]
    blocks = []
    for r in range(CHIPS):
        a, b = 2 * r + zl, 2 * r + 1 - zl
        blocks += [a, 15 - a, b, 15 - b]
    positions = (jnp.stack(own)[:, None] * BLK + jnp.arange(BLK, dtype=jnp.int32)[None, :]).reshape(CHIP)
    start = jnp.max(jnp.where(positions[:, None] >= ends[None, :], ends[None, :], 0), axis=1).astype(jnp.int32)
    start = start.reshape(4, 1, BLK)
    lowest = start[:, 0, 0] // PAIR_TOK
    where = jnp.stack(
        own
        + [jnp.minimum(lowest[0], lowest[2]), jnp.minimum(lowest[1], lowest[3]), x_at, role]
        + blocks
    ).astype(jnp.int32)
    own_table = jnp.concatenate([lax.dynamic_slice_in_dim(table, b * BLK, BLK, 0) for b in own], axis=0)

    n3 = after(n3, q_s, where, start, own_table)
    n_m = jnp.where(resident, n3, n2)
    q_m = q_call(jnp.stack([c, far, 15 - far]), n_m, w, table)
    g1, g2, q_m = lax.optimization_barrier((g1, g2, q_m))
    q = (q_s, q_m)
    do = (jnp.where(resident, g_mine, g1), jnp.where(resident, g1, g2))

    mine = after(jnp.where(resident, normed, n2), g1, g2)
    direct = {(4 - by) % 4: shift(mine, "x", by) for by in (2, 1, 3)}
    direct = [direct[r] for r in (1, 2, 3)]

    o_keep, o_give, dq, dq_to, dkv = attention_call(
        where, q, do, own_table, start, kv_all
    )

    dkv = lax.all_to_all(dkv, "y", 0, 0, tiled=True)
    dn_q = dnorm_q_call(sel, dq, w)
    jq = {(4 - by) % 4: shift(after(dq_to[by], *direct), "x", by) for by in (2, 1, 3)}
    jq = [dq_to[0], jq[1], jq[2], jq[3]]
    h1 = lax.ppermute(o_give, PAIR, RETURN1)
    h2 = lax.ppermute(o_keep, PAIR, SPREAD2)
    half_mine = jnp.where(resident, o_keep, h2)
    attended = jnp.concatenate(
        [jnp.where(zl == 0, half_mine, h1), jnp.where(zl == 0, h1, half_mine)], axis=1
    )

    via = [swap_cores(after(piece, dn_q, h2, *jq[1:])) for piece in direct]
    joined_kv, jkv_to = joined_call(x_at.reshape(1), after(dkv, dn_q, attended, *via), own_table)
    jkv = {(4 - by) % 4: shift(jkv_to[by], "x", by) for by in (2, 1, 3)}
    jkv = [jkv_to[0], jkv[1], jkv[2], jkv[3]]

    dn_keep, dn_give = dnorm_call(sel, dn_q, joined_kv, w)
    d1 = swap_cores(dn_give)
    summed = (dn_keep.astype(F32) + after(d1, *jkv).astype(F32)).astype(BF16)
    d2 = lax.ppermute(summed, PAIR, SPREAD2)
    parts = weight_call(after(sel, summed), (n_s, n_m), direct, via, jq, jkv)
    parts = lax.all_to_all(after(parts, d2).reshape(64, 2, 16, WCOLS), ("x", "zh", "y", "zl"), 0, 0, tiled=True)

    inputs_grad = inputs_call(sel, x, gain2, dn_keep, d1, d2)

    at = ((((x_at * 2 + zh) * 2 + c) * 4 + y) * 2 + zl) * 16
    w_rows = lax.dynamic_slice_in_dim(w, at, 16, 0)
    gain_rows = lax.dynamic_slice_in_dim(gain2, at, 16, 1)
    keep, give = sum_call(sel, after(parts, inputs_grad, w_rows, gain_rows))
    got = swap_cores(give)
    qkv_grad, gain_grad = finish_call(sel, keep, got, w_rows, gain_rows)
    return (
        attended.reshape(1, 2, 1, BLK, 2048),
        inputs_grad.reshape(1, 2, 1, BLK, D),
        qkv_grad,
        gain_grad.reshape(16),
    )


def solution(mesh):
    fine = Mesh(mesh.devices.reshape(4, 2, 2, 4, 2), ("x", "zh", "c", "y", "zl"))
    dp, ctx = ("x", "zh", "c"), ("y", "zl")
    rows = P(dp, None, ctx, None, None)
    return jax.shard_map(
        body,
        mesh=fine,
        in_specs=(rows, P(), P(), P(dp, None), rows),
        out_specs=(rows, rows, P(dp + ctx, None), P(dp + ctx)),
        check_vma=False,
    )
```

```python
import jax
import jax.numpy as jnp
import numpy as np
from jax import lax
from jax.experimental import pallas as pl
from jax.experimental.pallas import tpu as pltpu
from jax.sharding import Mesh
from jax.sharding import PartitionSpec as P

HEAD = 128
GROUP = 4
D = 2048
BLK = 128
TOK = 256
CHIP = 512
NBLK = 16
WCOLS = 384
CHIPS = 4
PAIR_TOK = 2 * BLK
COLS = 4 * PAIR_TOK
WINDOW = 5
EPS = 1e-05
ROPE_BASE = 500000.0
SCALE = HEAD ** (-0.5)
EXP2_SCALE = SCALE * 1.4426950408889634
F32, BF16 = jnp.float32, jnp.bfloat16
VMEM_LIMIT = 56 * 1024 * 1024

ANGLES = np.arange(2048)[:, None] * ROPE_BASE ** (-2.0 * np.arange(64) / HEAD)
TABLE = np.concatenate([np.cos(ANGLES)] * 2 + [-np.sin(ANGLES), np.sin(ANGLES)], axis=1).astype(np.float32)

SPREAD1 = [(0, 2), (3, 1), (1, 0), (2, 3)]
SPREAD2 = [(1, 2), (2, 1)]
RETURN1 = [(2, 0), (1, 3), (0, 1), (3, 2)]
HOME_TO_VISITOR = [(0, 2), (3, 1)]
VISITOR_ACROSS = [(1, 0), (2, 3)]
PAIR = ("c", "zl")


def cost(us):
    return pl.CostEstimate(flops=int(us * 10**6), bytes_accessed=int(us * (1 << 20)), transcendentals=0)


def params(limit=VMEM_LIMIT):
    return pltpu.CompilerParams(vmem_limit_bytes=limit)


def dot_nt(a, b):
    return lax.dot_general(a, b, (((1,), (1,)), ((), ())), preferred_element_type=F32)


def dot_tn(a, b):
    return lax.dot_general(a, b, (((0,), (0,)), ((), ())), preferred_element_type=F32)


def dot_nn(a, b):
    return lax.dot_general(a, b, (((1,), (0,)), ((), ())), preferred_element_type=F32)


def rotate(v, cos, sin):
    return v * cos + pltpu.roll(v, 64, 1) * sin


def kv_kernel(sel_ref, x_ref, gain_ref, wk_ref, wv_ref, ta_ref, tb_ref, normed_ref, mine_ref, other_ref):
    step = pl.program_id(0)

    @pl.when(step == 0)
    def _():
        x = x_ref[...].astype(F32)
        inv = lax.rsqrt(jnp.mean(x * x, axis=1, keepdims=True) + EPS)
        normed_ref[...] = ((x * inv) * gain_ref[...]).astype(BF16)

    keys = dot_nn(normed_ref[...], wk_ref[...])
    values = dot_nn(normed_ref[...], wv_ref[...]).astype(BF16)
    table = jnp.concatenate([ta_ref[...], tb_ref[...]], axis=0)
    cos, sin = table[:, :HEAD], table[:, HEAD:]
    keys = jnp.concatenate(
        [rotate(keys[:, i * HEAD : (i + 1) * HEAD], cos, sin).astype(BF16) for i in range(2)], axis=1
    )

    @pl.when(step == 0)
    def _():
        mine_ref[:, :256] = keys
        mine_ref[:, 256:] = values

    @pl.when(step == 1)
    def _():
        other_ref[:, :256] = keys
        other_ref[:, 256:] = values


def kv_call(sel, x, gain, w, table):
    half = jax.ShapeDtypeStruct((TOK, 512), BF16)
    return pl.pallas_call(
        kv_kernel,
        grid_spec=pltpu.PrefetchScalarGridSpec(
            num_scalar_prefetch=1,
            grid=(2,),
            in_specs=[
                pl.BlockSpec((TOK, D), lambda t, sel: (0, 0)),
                pl.BlockSpec((1, D), lambda t, sel: (0, 0)),
                pl.BlockSpec((D, 256), lambda t, sel: (0, 8 + (sel[0] + t) % 2)),
                pl.BlockSpec((D, 256), lambda t, sel: (0, 10 + (sel[0] + t) % 2)),
                pl.BlockSpec((BLK, 256), lambda t, sel: (sel[1], 0)),
                pl.BlockSpec((BLK, 256), lambda t, sel: (sel[2], 0)),
            ],
            out_specs=[
                pl.BlockSpec((TOK, D), lambda t, sel: (0, 0)),
                pl.BlockSpec((TOK, 512), lambda t, sel: (0, 0)),
                pl.BlockSpec((TOK, 512), lambda t, sel: (0, 0)),
            ],
        ),
        out_shape=[jax.ShapeDtypeStruct((TOK, D), BF16), half, half],
        compiler_params=params(),
        cost_estimate=cost(0.01),
        name="kv_home",
    )(sel, x, gain, w, w, table, table)


def q_kernel(sel_ref, n_ref, w_ref, ta_ref, tb_ref, q_ref):
    out = dot_nn(n_ref[...], w_ref[...])
    table = jnp.concatenate([ta_ref[...], tb_ref[...]], axis=0)
    for i in range(4):
        cols = slice(i * HEAD, (i + 1) * HEAD)
        q_ref[:, cols] = rotate(out[:, cols], table[:, :HEAD], table[:, HEAD:]).astype(BF16)


def q_call(sel, normed, w, table):
    return pl.pallas_call(
        q_kernel,
        grid_spec=pltpu.PrefetchScalarGridSpec(
            num_scalar_prefetch=1,
            grid=(2,),
            in_specs=[
                pl.BlockSpec((TOK, D), lambda t, sel: (0, 0)),
                pl.BlockSpec((D, 512), lambda t, sel: (0, sel[0] * 2 + t)),
                pl.BlockSpec((BLK, 256), lambda t, sel: (sel[1], 0)),
                pl.BlockSpec((BLK, 256), lambda t, sel: (sel[2], 0)),
            ],
            out_specs=pl.BlockSpec((TOK, 512), lambda t, sel: (0, t)),
        ),
        out_shape=jax.ShapeDtypeStruct((TOK, 1024), BF16),
        compiler_params=params(),
        cost_estimate=cost(0.1),
        name="q_proj",
    )(sel, normed, w, table, table)


def attention_kernel(
    where_ref, qs_ref, qm_ref, dos_ref, dom_ref, table_ref, start_ref, kv_ref,
    keep_ref, give_ref, dq_ref, x0, x1, x2, x3, dkv_ref, kvbuf, acc, score, quarters,
):
    home = where_ref[7] == 0
    for r in range(CHIPS):
        for part in range(2):
            for half in range(2):
                block = where_ref[8 + r * 4 + part * 2 + half]
                kvbuf[block] = kv_ref[r, part, half * BLK : (half + 1) * BLK, :]
    acc[...] = jnp.zeros_like(acc)
    row = lax.broadcasted_iota(jnp.int32, (PAIR_TOK, COLS), 0)
    for p in range(2):
        rows = slice(p * BLK, (p + 1) * BLK)
        heads = [[slice((h * GROUP + g) * HEAD, (h * GROUP + g + 1) * HEAD) for g in range(GROUP)] for h in range(2)]
        kc = [slice(h * HEAD, (h + 1) * HEAD) for h in range(2)]
        vc = [slice(256 + h * HEAD, 256 + (h + 1) * HEAD) for h in range(2)]
        queries = [jnp.concatenate([ref[rows, g] for ref in (qs_ref, qm_ref) for g in heads[h]], axis=0) for h in range(2)]
        grads = [jnp.concatenate([ref[rows, g] for ref in (dos_ref, dom_ref) for g in heads[h]], axis=0) for h in range(2)]
        first = where_ref[4 + p]
        count = where_ref[p] // 2 - first + 1
        start = jnp.concatenate([start_ref[p]] * GROUP + [start_ref[2 + p]] * GROUP, axis=1)
        token = lax.broadcasted_iota(jnp.int32, (1, GROUP * BLK), 1) % BLK
        pos = jnp.concatenate([where_ref[p] * BLK + token, where_ref[2 + p] * BLK + token], axis=1)

        def pair(i, cols):
            return jnp.concatenate([kvbuf[2 * i, :, cols], kvbuf[2 * i + 1, :, cols]], axis=0)

        def score_step(i, tops, first=first, kc=kc, queries=queries, start=start, pos=pos):
            at = (first + i) * PAIR_TOK + row
            allowed = (at >= start) & (at <= pos)
            out = []
            for h in range(2):
                s = dot_nt(pair(first + i, kc[h]), queries[h])
                s = jnp.where(allowed, s, -jnp.inf)
                score[h, i] = s
                out.append(jnp.maximum(tops[h], jnp.max(s.reshape(PAIR_TOK // 8, 8, COLS), axis=0)))
            return tuple(out)

        tops = lax.fori_loop(0, count, score_step, (jnp.full((8, COLS), -jnp.inf, F32),) * 2)
        tops = [jnp.max(t, axis=0, keepdims=True) * EXP2_SCALE for t in tops]

        def value_step(i, carry, first=first, vc=vc, tops=tops):
            res = []
            for h in range(2):
                total, out = carry[h]
                e = jnp.exp2(score[h, i] * EXP2_SCALE - tops[h])
                score[h, i] = e
                total = total + jnp.sum(e.reshape(PAIR_TOK // 8, 8, COLS), axis=0)
                out = out + dot_tn(pair(first + i, vc[h]), e.astype(BF16))
                res.append((total, out))
            return tuple(res)

        carry = lax.fori_loop(
            0, count, value_step, ((jnp.zeros((8, COLS), F32), jnp.zeros((HEAD, COLS), F32)),) * 2
        )
        invs, deltas = [], []
        for h in range(2):
            total, out = carry[h]
            inv = 1.0 / jnp.sum(total, axis=0, keepdims=True)
            out = (out * inv).astype(BF16).astype(F32)
            deltas.append(jnp.sum(out * grads[h].astype(F32).T, axis=0, keepdims=True))
            invs.append(inv)
            for g in range(GROUP):
                of_s = out[:, g * BLK : (g + 1) * BLK].T.astype(BF16)
                of_m = out[:, (GROUP + g) * BLK : (GROUP + g + 1) * BLK].T.astype(BF16)
                keep_ref[rows, heads[h][g]] = jnp.where(home, of_s, of_m)
                give_ref[rows, heads[h][g]] = jnp.where(home, of_m, of_s)

        def grad_step(i, dqs, first=first, kc=kc, vc=vc, invs=invs, deltas=deltas, queries=queries, grads=grads):
            res = []
            j = first + i
            for h in range(2):
                keys, values = pair(j, kc[h]), pair(j, vc[h])
                prob = score[h, i] * invs[h]
                dp = dot_nt(values, grads[h])
                ds = (prob * (dp - deltas[h])).astype(BF16)
                dv = dot_nn(prob.astype(BF16), grads[h])
                dk = dot_nn(ds, queries[h])
                for k in range(2):
                    acc[2 * j + k, :, vc[h]] += dv[k * BLK : (k + 1) * BLK]
                    acc[2 * j + k, :, kc[h]] += dk[k * BLK : (k + 1) * BLK]
                res.append(dqs[h] + dot_tn(keys, ds))
            return tuple(res)

        dqs = lax.fori_loop(0, count, grad_step, (jnp.zeros((HEAD, COLS), F32),) * 2)
        for k in range(2):
            at = (2 * k + p) * BLK
            rows = slice(at, at + BLK)
            cos, sin = table_ref[rows, :HEAD] * SCALE, table_ref[rows, HEAD:] * SCALE
            for h in range(2):
                for g in range(GROUP):
                    at = (k * GROUP + g) * BLK
                    part = rotate(dqs[h][:, at : at + BLK].T, cos, -sin).astype(BF16)
                    dq_ref[rows, heads[h][g]] = part
                    j = h * GROUP + g
                    quarters[j // 2, rows, (j % 2) * HEAD : (j % 2 + 1) * HEAD] = part
    for r, out in enumerate((x0, x1, x2, x3)):
        out[...] = quarters[(where_ref[6] + r) % 4]
    for r in range(CHIPS):
        for j in range(4):
            at, rows = where_ref[8 + r * 4 + j], slice(j * BLK, (j + 1) * BLK)
            dkv_ref[r, rows, :256] = (acc[at, :, :256] * SCALE).astype(BF16)
            dkv_ref[r, rows, 256:] = acc[at, :, 256:].astype(BF16)


def attention_call(where, q, do, table, start, kv):
    vmem = pl.BlockSpec(memory_space=pltpu.VMEM)
    half = jax.ShapeDtypeStruct((TOK, 1024), BF16)
    out = pl.pallas_call(
        attention_kernel,
        in_specs=[pl.BlockSpec(memory_space=pltpu.SMEM)] + [vmem] * 7,
        out_specs=[vmem] * 8,
        out_shape=[half, half, jax.ShapeDtypeStruct((CHIP, 1024), BF16)]
        + [jax.ShapeDtypeStruct((CHIP, 256), BF16)] * 4
        + [jax.ShapeDtypeStruct((CHIPS, CHIP, 512), BF16)],
        scratch_shapes=[
            pltpu.VMEM((NBLK, BLK, 512), BF16),
            pltpu.VMEM((NBLK, BLK, 512), F32),
            pltpu.VMEM((2, WINDOW, PAIR_TOK, COLS), F32),
            pltpu.VMEM((4, CHIP, 256), BF16),
        ],
        compiler_params=params(),
        cost_estimate=cost(0.1),
        name="attention",
    )(where, *q, *do, table, start, kv)
    return out[0], out[1], out[2], out[3:7], out[7]


def joined_kernel(x_ref, parts_ref, table_ref, out_ref, j0, j1, j2, j3):
    total = jnp.sum(parts_ref[...].astype(F32), axis=0)
    for i in range(2):
        cols = slice(i * HEAD, (i + 1) * HEAD)
        out_ref[:, cols] = rotate(total[:, cols], table_ref[:, :HEAD], -table_ref[:, HEAD:]).astype(BF16)
    out_ref[:, 256:] = total[:, 256:].astype(BF16)
    for r, out in enumerate((j0, j1, j2, j3)):
        out[...] = out_ref[:, pl.ds(pl.multiple_of((x_ref[0] + r) % 4 * HEAD, HEAD), HEAD)]


def joined_call(x_at, parts, table):
    vmem = pl.BlockSpec(memory_space=pltpu.VMEM)
    out = pl.pallas_call(
        joined_kernel,
        in_specs=[pl.BlockSpec(memory_space=pltpu.SMEM)] + [vmem] * 2,
        out_specs=[vmem] * 5,
        out_shape=[jax.ShapeDtypeStruct((CHIP, 512), BF16)] + [jax.ShapeDtypeStruct((CHIP, HEAD), BF16)] * 4,
        compiler_params=params(),
        cost_estimate=cost(0.1),
        name="joined_kv",
    )(x_at, parts, table)
    return out[0], out[1:]


def dnorm_q_kernel(sel_ref, j_ref, w_ref, out_ref):
    out_ref[...] = dot_nt(j_ref[...], w_ref[...]).astype(BF16)


def dnorm_q_call(sel, jq, w):
    tile = 512
    return pl.pallas_call(
        dnorm_q_kernel,
        grid_spec=pltpu.PrefetchScalarGridSpec(
            num_scalar_prefetch=1,
            grid=(D // tile,),
            in_specs=[
                pl.BlockSpec((CHIP, 1024), lambda t, sel: (0, 0)),
                pl.BlockSpec((tile, 1024), lambda t, sel: (t, sel[0])),
            ],
            out_specs=pl.BlockSpec((CHIP, tile), lambda t, sel: (0, t)),
        ),
        out_shape=jax.ShapeDtypeStruct((CHIP, D), BF16),
        compiler_params=params(),
        cost_estimate=cost(0.01),
        name="d_normed_q",
    )(sel, jq, w)


def dnorm_kernel(sel_ref, part_ref, jkv_ref, wk_ref, wv_ref, keep_ref, give_ref):
    out = part_ref[...].astype(F32)
    out += dot_nt(jkv_ref[:, :256], wk_ref[...])
    out += dot_nt(jkv_ref[:, 256:], wv_ref[...])
    home = sel_ref[1] == 0
    of_s, of_m = out[:TOK].astype(BF16), out[TOK:].astype(BF16)
    keep_ref[...] = jnp.where(home, of_s, of_m)
    give_ref[...] = jnp.where(home, of_m, of_s)


def dnorm_call(sel, part, jkv, w):
    tile = 1024
    return pl.pallas_call(
        dnorm_kernel,
        grid_spec=pltpu.PrefetchScalarGridSpec(
            num_scalar_prefetch=1,
            grid=(D // tile,),
            in_specs=[
                pl.BlockSpec((CHIP, tile), lambda t, sel: (0, t)),
                pl.BlockSpec((CHIP, 512), lambda t, sel: (0, 0)),
                pl.BlockSpec((tile, 256), lambda t, sel: (t, 8 + sel[0])),
                pl.BlockSpec((tile, 256), lambda t, sel: (t, 10 + sel[0])),
            ],
            out_specs=[pl.BlockSpec((TOK, tile), lambda t, sel: (0, t))] * 2,
        ),
        out_shape=[jax.ShapeDtypeStruct((TOK, D), BF16)] * 2,
        compiler_params=params(),
        cost_estimate=cost(0.01),
        name="d_normed",
    )(sel, part, jkv, w, w)


def weight_kernel(sel_ref, ns, nm, d1, d2, d3, v1, v2, v3, q0, q1, q2, q3, k0, k1, k2, k3, out_ref, jt):
    role = sel_ref[1]
    pieces = ((ns, q0, k0, 0), (nm, q0, k0, TOK))
    for direct, via, q, k in ((d1, v1, q1, k1), (d2, v2, q2, k2), (d3, v3, q3, k3)):
        pieces += ((direct, q, k, role * TOK), (via, q, k, (1 - role) * TOK))

    @pl.when(pl.program_id(0) == 0)
    def _():
        for i, (_, q, k, at) in enumerate(pieces):
            jt[:256, i * TOK : (i + 1) * TOK] = q[pl.ds(at, TOK), :].T
            jt[256:, i * TOK : (i + 1) * TOK] = k[pl.ds(at, TOK), :].T

    out = jnp.zeros((WCOLS, out_ref.shape[0] * TOK), F32)
    for i, (n, _, _, _) in enumerate(pieces):
        out += dot_nn(jt[:, i * TOK : (i + 1) * TOK], n[...])
    for t in range(out_ref.shape[0]):
        part = out[:, t * TOK : (t + 1) * TOK].T.astype(BF16)
        for i in range(2):
            for k in range(8):
                at = i * 128 + k * 16
                out_ref[t, k, i] = part[at : at + 16]


def weight_call(sel, tokens, direct, via, jq, jkv):
    tile = 512
    part = pl.BlockSpec((TOK, tile), lambda t, sel: (0, t))
    return pl.pallas_call(
        weight_kernel,
        grid_spec=pltpu.PrefetchScalarGridSpec(
            num_scalar_prefetch=1,
            grid=(D // tile,),
            in_specs=[part] * 8
            + [pl.BlockSpec((CHIP, 256), lambda t, sel: (0, 0))] * 4
            + [pl.BlockSpec((CHIP, HEAD), lambda t, sel: (0, 0))] * 4,
            out_specs=pl.BlockSpec((tile // TOK, 8, 2, 16, WCOLS), lambda t, sel: (t, 0, 0, 0, 0)),
            scratch_shapes=[pltpu.VMEM((WCOLS, 8 * TOK), BF16)],
        ),
        out_shape=jax.ShapeDtypeStruct((8, 8, 2, 16, WCOLS), BF16),
        compiler_params=params(24 * 1024 * 1024),
        cost_estimate=cost(0.1),
        name="weight_grad",
    )(sel, *tokens, *direct, *via, *jq, *jkv)


def sum_kernel(sel_ref, parts_ref, keep_ref, give_ref):
    core = sel_ref[0]
    for x in range(4):
        keep_ref[x] = jnp.sum(parts_ref[x * 16 : (x + 1) * 16, core].astype(F32), axis=0)
        give_ref[x] = jnp.sum(parts_ref[x * 16 : (x + 1) * 16, 1 - core].astype(F32), axis=0)


def sum_call(sel, parts):
    vmem = pl.BlockSpec(memory_space=pltpu.VMEM)
    out = jax.ShapeDtypeStruct((4, 16, WCOLS), F32)
    return pl.pallas_call(
        sum_kernel,
        in_specs=[pl.BlockSpec(memory_space=pltpu.SMEM), vmem],
        out_specs=[vmem] * 2,
        out_shape=[out, out],
        compiler_params=params(),
        cost_estimate=cost(0.1),
        name="weight_sum",
    )(sel, parts)


def finish_kernel(sel_ref, own, got, w_ref, gain_ref, grad_ref, gain_grad_ref):
    first = sel_ref[0] == 0
    for core in range(2):
        for x in range(4):
            value = jnp.where(first == (core == 0), own[x], got[x])
            at = core * 1024 + x * 256
            grad_ref[:, at : at + 256] = value[:, :256]
            at = 2048 + (x // 2) * 512 + core * 256 + (x % 2) * HEAD
            grad_ref[:, at : at + HEAD] = value[:, 256:]
    total = jnp.sum(w_ref[...].astype(F32) * grad_ref[...], axis=1, keepdims=True)
    gain_grad_ref[...] = jnp.broadcast_to(total, (16, HEAD)).T[:1] / gain_ref[...]


def finish_call(sel, own, got, w_rows, gain_rows):
    vmem = pl.BlockSpec(memory_space=pltpu.VMEM)
    return pl.pallas_call(
        finish_kernel,
        in_specs=[pl.BlockSpec(memory_space=pltpu.SMEM)] + [vmem] * 4,
        out_specs=[vmem] * 2,
        out_shape=[jax.ShapeDtypeStruct((16, 3072), F32), jax.ShapeDtypeStruct((1, 16), F32)],
        compiler_params=params(),
        cost_estimate=cost(0.1),
        name="finish",
    )(sel, own, got, w_rows, gain_rows)


def inputs_kernel(sel_ref, x_ref, gain_ref, keep_ref, near_ref, far_ref, out_ref):
    x = x_ref[...].astype(F32)
    inv = lax.rsqrt(jnp.mean(x * x, axis=1, keepdims=True) + EPS)
    unit = x * inv
    here = keep_ref[...].astype(F32) + near_ref[...].astype(F32)
    d_normed = jnp.where(sel_ref[1] == 0, here, far_ref[...].astype(F32))
    scaled = d_normed * gain_ref[...]
    mean = jnp.mean(scaled * unit, axis=1, keepdims=True)
    out_ref[...] = (inv * (scaled - unit * mean)).astype(BF16)


def inputs_call(sel, x, gain, keep, near, far):
    tile = 128
    rows = pl.BlockSpec((tile, D), lambda t, sel: (t, 0))
    return pl.pallas_call(
        inputs_kernel,
        grid_spec=pltpu.PrefetchScalarGridSpec(
            num_scalar_prefetch=1,
            grid=(TOK // tile,),
            in_specs=[rows, pl.BlockSpec((1, D), lambda t, sel: (0, 0)), rows, rows, rows],
            out_specs=rows,
        ),
        out_shape=jax.ShapeDtypeStruct((TOK, D), BF16),
        compiler_params=params(),
        cost_estimate=cost(0.1),
        name="inputs_grad",
    )(sel, x, gain, keep, near, far)


def shift(value, axis, by):
    return lax.ppermute(value, axis, [(i, (i + by) % 4) for i in range(4)])


def swap_cores(value):
    return lax.ppermute(value, "c", [(0, 1), (1, 0)])


def after(value, *others):
    return lax.optimization_barrier((value,) + others)[0]


def body(inputs, gain, w, doc_lengths, out_grad):
    c, zl, y, x_at, zh = (lax.axis_index(a).astype(jnp.int32) for a in ("c", "zl", "y", "x", "zh"))
    resident = c == zl
    role = jnp.where(resident, 0, 1).astype(jnp.int32)
    sel = jnp.stack([c, role])
    x = inputs.reshape(TOK, D)
    grads = out_grad.reshape(TOK, 2048)
    gain2 = gain.reshape(1, D)
    near, far = 2 * y + zl, 2 * y + 1 - zl
    table = jnp.asarray(TABLE)

    g_mine = lax.dynamic_slice_in_dim(grads, zl * 1024, 1024, 1)
    g_other = lax.dynamic_slice_in_dim(grads, (1 - zl) * 1024, 1024, 1)
    lengths = doc_lengths.reshape(16)
    lengths_near = lax.ppermute(lengths, PAIR, HOME_TO_VISITOR)

    normed, kv_mine, kv_other = kv_call(jnp.stack([zl, near, 15 - near]), x, gain2, w, table)

    r1 = lax.ppermute(after(kv_other, lengths_near), PAIR, SPREAD1)
    r2 = lax.ppermute(kv_mine, PAIR, SPREAD2)
    kv = jnp.stack([jnp.where(resident, kv_mine, r1), jnp.where(resident, r1, r2)])
    kv = jnp.broadcast_to(kv, (CHIPS,) + kv.shape)

    n1 = lax.ppermute(normed, PAIR, HOME_TO_VISITOR)
    sent = after(normed, kv, n1)
    kv_all = lax.all_to_all(after(kv, n1), "y", 0, 0, tiled=True)
    n2 = lax.ppermute(sent, PAIR, SPREAD2)
    n3 = lax.ppermute(sent, PAIR, VISITOR_ACROSS)
    n_s = jnp.where(resident, normed, n1)

    q_s = q_call(jnp.stack([c, near, 15 - near]), n_s, w, table)

    g1 = lax.ppermute(after(g_other, q_s), PAIR, SPREAD1)
    g2 = lax.ppermute(after(g_mine, q_s), PAIR, SPREAD2)

    lengths = jnp.where(resident, lengths, lengths_near)
    upto = jnp.arange(16)
    ends = jnp.sum(jnp.where(upto[None, :] <= upto[:, None], lengths[None, :], 0), axis=1)
    own = [near, 15 - near, far, 15 - far]
    blocks = []
    for r in range(CHIPS):
        a, b = 2 * r + zl, 2 * r + 1 - zl
        blocks += [a, 15 - a, b, 15 - b]
    positions = (jnp.stack(own)[:, None] * BLK + jnp.arange(BLK, dtype=jnp.int32)[None, :]).reshape(CHIP)
    start = jnp.max(jnp.where(positions[:, None] >= ends[None, :], ends[None, :], 0), axis=1).astype(jnp.int32)
    start = start.reshape(4, 1, BLK)
    lowest = start[:, 0, 0] // PAIR_TOK
    where = jnp.stack(
        own
        + [jnp.minimum(lowest[0], lowest[2]), jnp.minimum(lowest[1], lowest[3]), x_at, role]
        + blocks
    ).astype(jnp.int32)
    own_table = jnp.concatenate([lax.dynamic_slice_in_dim(table, b * BLK, BLK, 0) for b in own], axis=0)

    n3 = after(n3, q_s, where, start, own_table)
    n_m = jnp.where(resident, n3, n2)
    q_m = q_call(jnp.stack([c, far, 15 - far]), n_m, w, table)
    g1, g2, q_m = lax.optimization_barrier((g1, g2, q_m))
    q = (q_s, q_m)
    do = (jnp.where(resident, g_mine, g1), jnp.where(resident, g1, g2))

    mine = after(jnp.where(resident, normed, n2), g1, g2)
    direct = {(4 - by) % 4: shift(mine, "x", by) for by in (2, 1, 3)}
    direct = [direct[r] for r in (1, 2, 3)]

    o_keep, o_give, dq, dq_to, dkv = attention_call(
        where, q, do, own_table, start, kv_all
    )

    dkv = lax.all_to_all(dkv, "y", 0, 0, tiled=True)
    dn_q = dnorm_q_call(sel, dq, w)
    jq = {(4 - by) % 4: shift(after(dq_to[by], *direct), "x", by) for by in (2, 1, 3)}
    jq = [dq_to[0], jq[1], jq[2], jq[3]]
    h1 = lax.ppermute(o_give, PAIR, RETURN1)
    h2 = lax.ppermute(o_keep, PAIR, SPREAD2)
    half_mine = jnp.where(resident, o_keep, h2)
    attended = jnp.concatenate(
        [jnp.where(zl == 0, half_mine, h1), jnp.where(zl == 0, h1, half_mine)], axis=1
    )

    via = [swap_cores(after(piece, dn_q, h2, *jq[1:])) for piece in direct]
    joined_kv, jkv_to = joined_call(x_at.reshape(1), after(dkv, dn_q, attended, *via), own_table)
    jkv = {(4 - by) % 4: shift(jkv_to[by], "x", by) for by in (2, 1, 3)}
    jkv = [jkv_to[0], jkv[1], jkv[2], jkv[3]]

    dn_keep, dn_give = dnorm_call(sel, dn_q, joined_kv, w)
    d1 = swap_cores(dn_give)
    summed = (dn_keep.astype(F32) + after(d1, *jkv).astype(F32)).astype(BF16)
    d2 = lax.ppermute(summed, PAIR, SPREAD2)
    parts = weight_call(after(sel, summed), (n_s, n_m), direct, via, jq, jkv)
    parts = lax.all_to_all(after(parts, d2).reshape(64, 2, 16, WCOLS), ("x", "zh", "y", "zl"), 0, 0, tiled=True)

    inputs_grad = inputs_call(sel, x, gain2, dn_keep, d1, d2)

    at = ((((x_at * 2 + zh) * 2 + c) * 4 + y) * 2 + zl) * 16
    w_rows = lax.dynamic_slice_in_dim(w, at, 16, 0)
    gain_rows = lax.dynamic_slice_in_dim(gain2, at, 16, 1)
    keep, give = sum_call(sel, after(parts, inputs_grad, w_rows, gain_rows))
    got = swap_cores(give)
    qkv_grad, gain_grad = finish_call(sel, keep, got, w_rows, gain_rows)
    return (
        attended.reshape(1, 2, 1, BLK, 2048),
        inputs_grad.reshape(1, 2, 1, BLK, D),
        qkv_grad,
        gain_grad.reshape(16),
    )


def solution(mesh):
    fine = Mesh(mesh.devices.reshape(4, 2, 2, 4, 2), ("x", "zh", "c", "y", "zl"))
    dp, ctx = ("x", "zh", "c"), ("y", "zl")
    rows = P(dp, None, ctx, None, None)
    return jax.shard_map(
        body,
        mesh=fine,
        in_specs=(rows, P(), P(), P(dp, None), rows),
        out_specs=(rows, rows, P(dp + ctx, None), P(dp + ctx)),
        check_vma=False,
    )
```

```python
import jax
import jax.numpy as jnp
import numpy as np
from jax import lax
from jax.experimental import pallas as pl
from jax.experimental.pallas import tpu as pltpu
from jax.sharding import Mesh
from jax.sharding import PartitionSpec as P

HEAD = 128
GROUP = 4
D = 2048
BLK = 128
TOK = 256
CHIP = 512
NBLK = 16
WCOLS = 384
CHIPS = 4
PAIR_TOK = 2 * BLK
COLS = 4 * PAIR_TOK
WINDOW = 5
EPS = 1e-05
ROPE_BASE = 500000.0
SCALE = HEAD ** (-0.5)
EXP2_SCALE = SCALE * 1.4426950408889634
F32, BF16 = jnp.float32, jnp.bfloat16
VMEM_LIMIT = 56 * 1024 * 1024

ANGLES = np.arange(2048)[:, None] * ROPE_BASE ** (-2.0 * np.arange(64) / HEAD)
TABLE = np.concatenate([np.cos(ANGLES)] * 2 + [-np.sin(ANGLES), np.sin(ANGLES)], axis=1).astype(np.float32)

SPREAD1 = [(0, 2), (3, 1), (1, 0), (2, 3)]
SPREAD2 = [(1, 2), (2, 1)]
RETURN1 = [(2, 0), (1, 3), (0, 1), (3, 2)]
HOME_TO_VISITOR = [(0, 2), (3, 1)]
VISITOR_ACROSS = [(1, 0), (2, 3)]
PAIR = ("c", "zl")


def cost(us):
    return pl.CostEstimate(flops=int(us * 10**6), bytes_accessed=int(us * (1 << 20)), transcendentals=0)


def params():
    return pltpu.CompilerParams(vmem_limit_bytes=VMEM_LIMIT)


def dot_nt(a, b):
    return lax.dot_general(a, b, (((1,), (1,)), ((), ())), preferred_element_type=F32)


def dot_tn(a, b):
    return lax.dot_general(a, b, (((0,), (0,)), ((), ())), preferred_element_type=F32)


def dot_nn(a, b):
    return lax.dot_general(a, b, (((1,), (0,)), ((), ())), preferred_element_type=F32)


def rotate(v, cos, sin):
    return v * cos + pltpu.roll(v, 64, 1) * sin


def kv_kernel(sel_ref, x_ref, gain_ref, wk_ref, wv_ref, ta_ref, tb_ref, normed_ref, mine_ref, other_ref):
    step = pl.program_id(0)

    @pl.when(step == 0)
    def _():
        x = x_ref[...].astype(F32)
        inv = lax.rsqrt(jnp.mean(x * x, axis=1, keepdims=True) + EPS)
        normed_ref[...] = ((x * inv) * gain_ref[...]).astype(BF16)

    keys = dot_nn(normed_ref[...], wk_ref[...])
    values = dot_nn(normed_ref[...], wv_ref[...]).astype(BF16)
    table = jnp.concatenate([ta_ref[...], tb_ref[...]], axis=0)
    cos, sin = table[:, :HEAD], table[:, HEAD:]
    keys = jnp.concatenate(
        [rotate(keys[:, i * HEAD : (i + 1) * HEAD], cos, sin).astype(BF16) for i in range(2)], axis=1
    )

    @pl.when(step == 0)
    def _():
        mine_ref[:, :256] = keys
        mine_ref[:, 256:] = values

    @pl.when(step == 1)
    def _():
        other_ref[:, :256] = keys
        other_ref[:, 256:] = values


def kv_call(sel, x, gain, w, table):
    half = jax.ShapeDtypeStruct((TOK, 512), BF16)
    return pl.pallas_call(
        kv_kernel,
        grid_spec=pltpu.PrefetchScalarGridSpec(
            num_scalar_prefetch=1,
            grid=(2,),
            in_specs=[
                pl.BlockSpec((TOK, D), lambda t, sel: (0, 0)),
                pl.BlockSpec((1, D), lambda t, sel: (0, 0)),
                pl.BlockSpec((D, 256), lambda t, sel: (0, 8 + (sel[0] + t) % 2)),
                pl.BlockSpec((D, 256), lambda t, sel: (0, 10 + (sel[0] + t) % 2)),
                pl.BlockSpec((BLK, 256), lambda t, sel: (sel[1], 0)),
                pl.BlockSpec((BLK, 256), lambda t, sel: (sel[2], 0)),
            ],
            out_specs=[
                pl.BlockSpec((TOK, D), lambda t, sel: (0, 0)),
                pl.BlockSpec((TOK, 512), lambda t, sel: (0, 0)),
                pl.BlockSpec((TOK, 512), lambda t, sel: (0, 0)),
            ],
        ),
        out_shape=[jax.ShapeDtypeStruct((TOK, D), BF16), half, half],
        compiler_params=params(),
        cost_estimate=cost(0.01),
        name="kv_home",
    )(sel, x, gain, w, w, table, table)


def q_kernel(sel_ref, n_ref, w_ref, ta_ref, tb_ref, q_ref):
    out = dot_nn(n_ref[...], w_ref[...])
    table = jnp.concatenate([ta_ref[...], tb_ref[...]], axis=0)
    for i in range(4):
        cols = slice(i * HEAD, (i + 1) * HEAD)
        q_ref[:, cols] = rotate(out[:, cols], table[:, :HEAD], table[:, HEAD:]).astype(BF16)


def q_call(sel, normed, w, table):
    return pl.pallas_call(
        q_kernel,
        grid_spec=pltpu.PrefetchScalarGridSpec(
            num_scalar_prefetch=1,
            grid=(2,),
            in_specs=[
                pl.BlockSpec((TOK, D), lambda t, sel: (0, 0)),
                pl.BlockSpec((D, 512), lambda t, sel: (0, sel[0] * 2 + t)),
                pl.BlockSpec((BLK, 256), lambda t, sel: (sel[1], 0)),
                pl.BlockSpec((BLK, 256), lambda t, sel: (sel[2], 0)),
            ],
            out_specs=pl.BlockSpec((TOK, 512), lambda t, sel: (0, t)),
        ),
        out_shape=jax.ShapeDtypeStruct((TOK, 1024), BF16),
        compiler_params=params(),
        cost_estimate=cost(0.1),
        name="q_proj",
    )(sel, normed, w, table, table)


def attention_kernel(
    where_ref, qs_ref, qm_ref, dos_ref, dom_ref, table_ref, start_ref, kv_ref,
    keep_ref, give_ref, dq_ref, x0, x1, x2, x3, dkv_ref, kvbuf, acc, score, quarters,
):
    home = where_ref[7] == 0
    for r in range(CHIPS):
        for part in range(2):
            for half in range(2):
                block = where_ref[8 + r * 4 + part * 2 + half]
                kvbuf[block] = kv_ref[r, part, half * BLK : (half + 1) * BLK, :]
    acc[...] = jnp.zeros_like(acc)
    row = lax.broadcasted_iota(jnp.int32, (PAIR_TOK, COLS), 0)
    for p in range(2):
        rows = slice(p * BLK, (p + 1) * BLK)
        heads = [[slice((h * GROUP + g) * HEAD, (h * GROUP + g + 1) * HEAD) for g in range(GROUP)] for h in range(2)]
        kc = [slice(h * HEAD, (h + 1) * HEAD) for h in range(2)]
        vc = [slice(256 + h * HEAD, 256 + (h + 1) * HEAD) for h in range(2)]
        queries = [jnp.concatenate([ref[rows, g] for ref in (qs_ref, qm_ref) for g in heads[h]], axis=0) for h in range(2)]
        grads = [jnp.concatenate([ref[rows, g] for ref in (dos_ref, dom_ref) for g in heads[h]], axis=0) for h in range(2)]
        first = where_ref[4 + p]
        count = where_ref[p] // 2 - first + 1
        start = jnp.concatenate([start_ref[p]] * GROUP + [start_ref[2 + p]] * GROUP, axis=1)
        token = lax.broadcasted_iota(jnp.int32, (1, GROUP * BLK), 1) % BLK
        pos = jnp.concatenate([where_ref[p] * BLK + token, where_ref[2 + p] * BLK + token], axis=1)

        def pair(i, cols):
            return jnp.concatenate([kvbuf[2 * i, :, cols], kvbuf[2 * i + 1, :, cols]], axis=0)

        def score_step(i, tops, first=first, kc=kc, queries=queries, start=start, pos=pos):
            at = (first + i) * PAIR_TOK + row
            allowed = (at >= start) & (at <= pos)
            out = []
            for h in range(2):
                s = dot_nt(pair(first + i, kc[h]), queries[h])
                s = jnp.where(allowed, s, -jnp.inf)
                score[h, i] = s
                out.append(jnp.maximum(tops[h], jnp.max(s.reshape(PAIR_TOK // 8, 8, COLS), axis=0)))
            return tuple(out)

        tops = lax.fori_loop(0, count, score_step, (jnp.full((8, COLS), -jnp.inf, F32),) * 2)
        tops = [jnp.max(t, axis=0, keepdims=True) * EXP2_SCALE for t in tops]

        def value_step(i, carry, first=first, vc=vc, tops=tops):
            res = []
            for h in range(2):
                total, out = carry[h]
                e = jnp.exp2(score[h, i] * EXP2_SCALE - tops[h])
                score[h, i] = e
                total = total + jnp.sum(e.reshape(PAIR_TOK // 8, 8, COLS), axis=0)
                out = out + dot_tn(pair(first + i, vc[h]), e.astype(BF16))
                res.append((total, out))
            return tuple(res)

        carry = lax.fori_loop(
            0, count, value_step, ((jnp.zeros((8, COLS), F32), jnp.zeros((HEAD, COLS), F32)),) * 2
        )
        invs, deltas = [], []
        for h in range(2):
            total, out = carry[h]
            inv = 1.0 / jnp.sum(total, axis=0, keepdims=True)
            out = (out * inv).astype(BF16).astype(F32)
            deltas.append(jnp.sum(out * grads[h].astype(F32).T, axis=0, keepdims=True))
            invs.append(inv)
            for g in range(GROUP):
                of_s = out[:, g * BLK : (g + 1) * BLK].T.astype(BF16)
                of_m = out[:, (GROUP + g) * BLK : (GROUP + g + 1) * BLK].T.astype(BF16)
                keep_ref[rows, heads[h][g]] = jnp.where(home, of_s, of_m)
                give_ref[rows, heads[h][g]] = jnp.where(home, of_m, of_s)

        def grad_step(i, dqs, first=first, kc=kc, vc=vc, invs=invs, deltas=deltas, queries=queries, grads=grads):
            res = []
            j = first + i
            for h in range(2):
                keys, values = pair(j, kc[h]), pair(j, vc[h])
                prob = score[h, i] * invs[h]
                dp = dot_nt(values, grads[h])
                ds = (prob * (dp - deltas[h])).astype(BF16)
                dv = dot_nn(prob.astype(BF16), grads[h])
                dk = dot_nn(ds, queries[h])
                for k in range(2):
                    acc[2 * j + k, :, vc[h]] += dv[k * BLK : (k + 1) * BLK]
                    acc[2 * j + k, :, kc[h]] += dk[k * BLK : (k + 1) * BLK]
                res.append(dqs[h] + dot_tn(keys, ds))
            return tuple(res)

        dqs = lax.fori_loop(0, count, grad_step, (jnp.zeros((HEAD, COLS), F32),) * 2)
        for k in range(2):
            at = (2 * k + p) * BLK
            rows = slice(at, at + BLK)
            cos, sin = table_ref[rows, :HEAD] * SCALE, table_ref[rows, HEAD:] * SCALE
            for h in range(2):
                for g in range(GROUP):
                    at = (k * GROUP + g) * BLK
                    part = rotate(dqs[h][:, at : at + BLK].T, cos, -sin).astype(BF16)
                    dq_ref[rows, heads[h][g]] = part
                    j = h * GROUP + g
                    quarters[j // 2, rows, (j % 2) * HEAD : (j % 2 + 1) * HEAD] = part
    for r, out in enumerate((x0, x1, x2, x3)):
        out[...] = quarters[(where_ref[6] + r) % 4]
    for r in range(CHIPS):
        for j in range(4):
            at, rows = where_ref[8 + r * 4 + j], slice(j * BLK, (j + 1) * BLK)
            dkv_ref[r, rows, :256] = (acc[at, :, :256] * SCALE).astype(BF16)
            dkv_ref[r, rows, 256:] = acc[at, :, 256:].astype(BF16)


def attention_call(where, q, do, table, start, kv):
    vmem = pl.BlockSpec(memory_space=pltpu.VMEM)
    half = jax.ShapeDtypeStruct((TOK, 1024), BF16)
    out = pl.pallas_call(
        attention_kernel,
        in_specs=[pl.BlockSpec(memory_space=pltpu.SMEM)] + [vmem] * 7,
        out_specs=[vmem] * 8,
        out_shape=[half, half, jax.ShapeDtypeStruct((CHIP, 1024), BF16)]
        + [jax.ShapeDtypeStruct((CHIP, 256), BF16)] * 4
        + [jax.ShapeDtypeStruct((CHIPS, CHIP, 512), BF16)],
        scratch_shapes=[
            pltpu.VMEM((NBLK, BLK, 512), BF16),
            pltpu.VMEM((NBLK, BLK, 512), F32),
            pltpu.VMEM((2, WINDOW, PAIR_TOK, COLS), F32),
            pltpu.VMEM((4, CHIP, 256), BF16),
        ],
        compiler_params=params(),
        cost_estimate=cost(0.1),
        name="attention",
    )(where, *q, *do, table, start, kv)
    return out[0], out[1], out[2], out[3:7], out[7]


def joined_kernel(x_ref, parts_ref, table_ref, out_ref, j0, j1, j2, j3):
    total = jnp.sum(parts_ref[...].astype(F32), axis=0)
    for i in range(2):
        cols = slice(i * HEAD, (i + 1) * HEAD)
        out_ref[:, cols] = rotate(total[:, cols], table_ref[:, :HEAD], -table_ref[:, HEAD:]).astype(BF16)
    out_ref[:, 256:] = total[:, 256:].astype(BF16)
    for r, out in enumerate((j0, j1, j2, j3)):
        out[...] = out_ref[:, pl.ds(pl.multiple_of((x_ref[0] + r) % 4 * HEAD, HEAD), HEAD)]


def joined_call(x_at, parts, table):
    vmem = pl.BlockSpec(memory_space=pltpu.VMEM)
    out = pl.pallas_call(
        joined_kernel,
        in_specs=[pl.BlockSpec(memory_space=pltpu.SMEM)] + [vmem] * 2,
        out_specs=[vmem] * 5,
        out_shape=[jax.ShapeDtypeStruct((CHIP, 512), BF16)] + [jax.ShapeDtypeStruct((CHIP, HEAD), BF16)] * 4,
        compiler_params=params(),
        cost_estimate=cost(0.1),
        name="joined_kv",
    )(x_at, parts, table)
    return out[0], out[1:]


def dnorm_q_kernel(sel_ref, j_ref, w_ref, out_ref):
    out_ref[...] = dot_nt(j_ref[...], w_ref[...]).astype(BF16)


def dnorm_q_call(sel, jq, w):
    tile = 512
    return pl.pallas_call(
        dnorm_q_kernel,
        grid_spec=pltpu.PrefetchScalarGridSpec(
            num_scalar_prefetch=1,
            grid=(D // tile,),
            in_specs=[
                pl.BlockSpec((CHIP, 1024), lambda t, sel: (0, 0)),
                pl.BlockSpec((tile, 1024), lambda t, sel: (t, sel[0])),
            ],
            out_specs=pl.BlockSpec((CHIP, tile), lambda t, sel: (0, t)),
        ),
        out_shape=jax.ShapeDtypeStruct((CHIP, D), BF16),
        compiler_params=params(),
        cost_estimate=cost(0.01),
        name="d_normed_q",
    )(sel, jq, w)


def dnorm_kernel(sel_ref, part_ref, jkv_ref, wk_ref, wv_ref, keep_ref, give_ref):
    out = part_ref[...].astype(F32)
    out += dot_nt(jkv_ref[:, :256], wk_ref[...])
    out += dot_nt(jkv_ref[:, 256:], wv_ref[...])
    home = sel_ref[1] == 0
    of_s, of_m = out[:TOK].astype(BF16), out[TOK:].astype(BF16)
    keep_ref[...] = jnp.where(home, of_s, of_m)
    give_ref[...] = jnp.where(home, of_m, of_s)


def dnorm_call(sel, part, jkv, w):
    tile = 1024
    return pl.pallas_call(
        dnorm_kernel,
        grid_spec=pltpu.PrefetchScalarGridSpec(
            num_scalar_prefetch=1,
            grid=(D // tile,),
            in_specs=[
                pl.BlockSpec((CHIP, tile), lambda t, sel: (0, t)),
                pl.BlockSpec((CHIP, 512), lambda t, sel: (0, 0)),
                pl.BlockSpec((tile, 256), lambda t, sel: (t, 8 + sel[0])),
                pl.BlockSpec((tile, 256), lambda t, sel: (t, 10 + sel[0])),
            ],
            out_specs=[pl.BlockSpec((TOK, tile), lambda t, sel: (0, t))] * 2,
        ),
        out_shape=[jax.ShapeDtypeStruct((TOK, D), BF16)] * 2,
        compiler_params=params(),
        cost_estimate=cost(0.01),
        name="d_normed",
    )(sel, part, jkv, w, w)


def weight_kernel(sel_ref, ns, nm, d1, d2, d3, v1, v2, v3, q0, q1, q2, q3, k0, k1, k2, k3, out_ref, jt):
    role = sel_ref[1]
    pieces = ((ns, q0, k0, 0), (nm, q0, k0, TOK))
    for direct, via, q, k in ((d1, v1, q1, k1), (d2, v2, q2, k2), (d3, v3, q3, k3)):
        pieces += ((direct, q, k, role * TOK), (via, q, k, (1 - role) * TOK))

    @pl.when(pl.program_id(0) == 0)
    def _():
        for i, (_, q, k, at) in enumerate(pieces):
            jt[:256, i * TOK : (i + 1) * TOK] = q[pl.ds(at, TOK), :].T
            jt[256:, i * TOK : (i + 1) * TOK] = k[pl.ds(at, TOK), :].T

    out = jnp.zeros((WCOLS, out_ref.shape[0] * TOK), F32)
    for i, (n, _, _, _) in enumerate(pieces):
        out += dot_nn(jt[:, i * TOK : (i + 1) * TOK], n[...])
    for t in range(out_ref.shape[0]):
        part = out[:, t * TOK : (t + 1) * TOK].T.astype(BF16)
        for i in range(2):
            for k in range(8):
                at = i * 128 + k * 16
                out_ref[t, k, i] = part[at : at + 16]


def weight_call(sel, tokens, direct, via, jq, jkv):
    tile = 512
    part = pl.BlockSpec((TOK, tile), lambda t, sel: (0, t))
    return pl.pallas_call(
        weight_kernel,
        grid_spec=pltpu.PrefetchScalarGridSpec(
            num_scalar_prefetch=1,
            grid=(D // tile,),
            in_specs=[part] * 8
            + [pl.BlockSpec((CHIP, 256), lambda t, sel: (0, 0))] * 4
            + [pl.BlockSpec((CHIP, HEAD), lambda t, sel: (0, 0))] * 4,
            out_specs=pl.BlockSpec((tile // TOK, 8, 2, 16, WCOLS), lambda t, sel: (t, 0, 0, 0, 0)),
            scratch_shapes=[pltpu.VMEM((WCOLS, 8 * TOK), BF16)],
        ),
        out_shape=jax.ShapeDtypeStruct((8, 8, 2, 16, WCOLS), BF16),
        compiler_params=params(),
        cost_estimate=cost(0.1),
        name="weight_grad",
    )(sel, *tokens, *direct, *via, *jq, *jkv)


def sum_kernel(sel_ref, parts_ref, keep_ref, give_ref):
    core = sel_ref[0]
    for x in range(4):
        keep_ref[x] = jnp.sum(parts_ref[x * 16 : (x + 1) * 16, core].astype(F32), axis=0)
        give_ref[x] = jnp.sum(parts_ref[x * 16 : (x + 1) * 16, 1 - core].astype(F32), axis=0)


def sum_call(sel, parts):
    vmem = pl.BlockSpec(memory_space=pltpu.VMEM)
    out = jax.ShapeDtypeStruct((4, 16, WCOLS), F32)
    return pl.pallas_call(
        sum_kernel,
        in_specs=[pl.BlockSpec(memory_space=pltpu.SMEM), vmem],
        out_specs=[vmem] * 2,
        out_shape=[out, out],
        compiler_params=params(),
        cost_estimate=cost(0.1),
        name="weight_sum",
    )(sel, parts)


def finish_kernel(sel_ref, own, got, w_ref, gain_ref, grad_ref, gain_grad_ref):
    first = sel_ref[0] == 0
    for core in range(2):
        for x in range(4):
            value = jnp.where(first == (core == 0), own[x], got[x])
            at = core * 1024 + x * 256
            grad_ref[:, at : at + 256] = value[:, :256]
            at = 2048 + (x // 2) * 512 + core * 256 + (x % 2) * HEAD
            grad_ref[:, at : at + HEAD] = value[:, 256:]
    total = jnp.sum(w_ref[...].astype(F32) * grad_ref[...], axis=1, keepdims=True)
    gain_grad_ref[...] = jnp.broadcast_to(total, (16, HEAD)).T[:1] / gain_ref[...]


def finish_call(sel, own, got, w_rows, gain_rows):
    vmem = pl.BlockSpec(memory_space=pltpu.VMEM)
    return pl.pallas_call(
        finish_kernel,
        in_specs=[pl.BlockSpec(memory_space=pltpu.SMEM)] + [vmem] * 4,
        out_specs=[vmem] * 2,
        out_shape=[jax.ShapeDtypeStruct((16, 3072), F32), jax.ShapeDtypeStruct((1, 16), F32)],
        compiler_params=params(),
        cost_estimate=cost(0.1),
        name="finish",
    )(sel, own, got, w_rows, gain_rows)


def inputs_kernel(sel_ref, x_ref, gain_ref, keep_ref, near_ref, far_ref, out_ref):
    x = x_ref[...].astype(F32)
    inv = lax.rsqrt(jnp.mean(x * x, axis=1, keepdims=True) + EPS)
    unit = x * inv
    here = keep_ref[...].astype(F32) + near_ref[...].astype(F32)
    d_normed = jnp.where(sel_ref[1] == 0, here, far_ref[...].astype(F32))
    scaled = d_normed * gain_ref[...]
    mean = jnp.mean(scaled * unit, axis=1, keepdims=True)
    out_ref[...] = (inv * (scaled - unit * mean)).astype(BF16)


def inputs_call(sel, x, gain, keep, near, far):
    tile = 128
    rows = pl.BlockSpec((tile, D), lambda t, sel: (t, 0))
    return pl.pallas_call(
        inputs_kernel,
        grid_spec=pltpu.PrefetchScalarGridSpec(
            num_scalar_prefetch=1,
            grid=(TOK // tile,),
            in_specs=[rows, pl.BlockSpec((1, D), lambda t, sel: (0, 0)), rows, rows, rows],
            out_specs=rows,
        ),
        out_shape=jax.ShapeDtypeStruct((TOK, D), BF16),
        compiler_params=params(),
        cost_estimate=cost(0.1),
        name="inputs_grad",
    )(sel, x, gain, keep, near, far)


def shift(value, axis, by):
    return lax.ppermute(value, axis, [(i, (i + by) % 4) for i in range(4)])


def swap_cores(value):
    return lax.ppermute(value, "c", [(0, 1), (1, 0)])


def after(value, *others):
    return lax.optimization_barrier((value,) + others)[0]


def body(inputs, gain, w, doc_lengths, out_grad):
    c, zl, y, x_at, zh = (lax.axis_index(a).astype(jnp.int32) for a in ("c", "zl", "y", "x", "zh"))
    resident = c == zl
    role = jnp.where(resident, 0, 1).astype(jnp.int32)
    sel = jnp.stack([c, role])
    x = inputs.reshape(TOK, D)
    grads = out_grad.reshape(TOK, 2048)
    gain2 = gain.reshape(1, D)
    near, far = 2 * y + zl, 2 * y + 1 - zl
    table = jnp.asarray(TABLE)

    g_mine = lax.dynamic_slice_in_dim(grads, zl * 1024, 1024, 1)
    g_other = lax.dynamic_slice_in_dim(grads, (1 - zl) * 1024, 1024, 1)
    lengths = doc_lengths.reshape(16)
    lengths_near = lax.ppermute(lengths, PAIR, HOME_TO_VISITOR)

    normed, kv_mine, kv_other = kv_call(jnp.stack([zl, near, 15 - near]), x, gain2, w, table)

    r1 = lax.ppermute(after(kv_other, lengths_near), PAIR, SPREAD1)
    r2 = lax.ppermute(kv_mine, PAIR, SPREAD2)
    kv = jnp.stack([jnp.where(resident, kv_mine, r1), jnp.where(resident, r1, r2)])
    kv = jnp.broadcast_to(kv, (CHIPS,) + kv.shape)

    n1 = lax.ppermute(normed, PAIR, HOME_TO_VISITOR)
    sent = after(normed, kv, n1)
    kv_all = lax.all_to_all(after(kv, n1), "y", 0, 0, tiled=True)
    n2 = lax.ppermute(sent, PAIR, SPREAD2)
    n3 = lax.ppermute(sent, PAIR, VISITOR_ACROSS)
    n_s = jnp.where(resident, normed, n1)

    q_s = q_call(jnp.stack([c, near, 15 - near]), n_s, w, table)

    g1 = lax.ppermute(after(g_other, q_s), PAIR, SPREAD1)
    g2 = lax.ppermute(after(g_mine, q_s), PAIR, SPREAD2)

    lengths = jnp.where(resident, lengths, lengths_near)
    upto = jnp.arange(16)
    ends = jnp.sum(jnp.where(upto[None, :] <= upto[:, None], lengths[None, :], 0), axis=1)
    own = [near, 15 - near, far, 15 - far]
    blocks = []
    for r in range(CHIPS):
        a, b = 2 * r + zl, 2 * r + 1 - zl
        blocks += [a, 15 - a, b, 15 - b]
    positions = (jnp.stack(own)[:, None] * BLK + jnp.arange(BLK, dtype=jnp.int32)[None, :]).reshape(CHIP)
    start = jnp.max(jnp.where(positions[:, None] >= ends[None, :], ends[None, :], 0), axis=1).astype(jnp.int32)
    start = start.reshape(4, 1, BLK)
    lowest = start[:, 0, 0] // PAIR_TOK
    where = jnp.stack(
        own
        + [jnp.minimum(lowest[0], lowest[2]), jnp.minimum(lowest[1], lowest[3]), x_at, role]
        + blocks
    ).astype(jnp.int32)
    own_table = jnp.concatenate([lax.dynamic_slice_in_dim(table, b * BLK, BLK, 0) for b in own], axis=0)

    n3 = after(n3, q_s, where, start, own_table)
    n_m = jnp.where(resident, n3, n2)
    q_m = q_call(jnp.stack([c, far, 15 - far]), n_m, w, table)
    g1, g2, q_m = lax.optimization_barrier((g1, g2, q_m))
    q = (q_s, q_m)
    do = (jnp.where(resident, g_mine, g1), jnp.where(resident, g1, g2))

    mine = after(jnp.where(resident, normed, n2), g1, g2)
    direct = {(4 - by) % 4: shift(mine, "x", by) for by in (2, 1, 3)}
    direct = [direct[r] for r in (1, 2, 3)]

    o_keep, o_give, dq, dq_to, dkv = attention_call(
        where, q, do, own_table, start, kv_all
    )

    dkv = lax.all_to_all(dkv, "y", 0, 0, tiled=True)
    dn_q = dnorm_q_call(sel, dq, w)
    jq = {(4 - by) % 4: shift(after(dq_to[by], *direct), "x", by) for by in (2, 1, 3)}
    jq = [dq_to[0], jq[1], jq[2], jq[3]]
    h1 = lax.ppermute(o_give, PAIR, RETURN1)
    h2 = lax.ppermute(o_keep, PAIR, SPREAD2)
    half_mine = jnp.where(resident, o_keep, h2)
    attended = jnp.concatenate(
        [jnp.where(zl == 0, half_mine, h1), jnp.where(zl == 0, h1, half_mine)], axis=1
    )

    via = [swap_cores(after(piece, dn_q, h2, *jq[1:])) for piece in direct]
    joined_kv, jkv_to = joined_call(x_at.reshape(1), after(dkv, dn_q, attended, *via), own_table)
    jkv = {(4 - by) % 4: shift(jkv_to[by], "x", by) for by in (2, 1, 3)}
    jkv = [jkv_to[0], jkv[1], jkv[2], jkv[3]]

    parts = weight_call(sel, (n_s, n_m), direct, via, jq, jkv)
    dn_keep, dn_give = dnorm_call(sel, after(dn_q, parts), joined_kv, w)
    d1 = swap_cores(dn_give)
    summed = (dn_keep.astype(F32) + d1.astype(F32)).astype(BF16)
    d2 = lax.ppermute(summed, PAIR, SPREAD2)
    parts = lax.all_to_all(parts.reshape(64, 2, 16, WCOLS), ("x", "zh", "y", "zl"), 0, 0, tiled=True)

    inputs_grad = inputs_call(sel, x, gain2, dn_keep, d1, d2)

    at = ((((x_at * 2 + zh) * 2 + c) * 4 + y) * 2 + zl) * 16
    w_rows = lax.dynamic_slice_in_dim(w, at, 16, 0)
    gain_rows = lax.dynamic_slice_in_dim(gain2, at, 16, 1)
    keep, give = sum_call(sel, after(parts, w_rows, gain_rows))
    got = swap_cores(give)
    qkv_grad, gain_grad = finish_call(sel, keep, got, w_rows, gain_rows)
    return (
        attended.reshape(1, 2, 1, BLK, 2048),
        inputs_grad.reshape(1, 2, 1, BLK, D),
        qkv_grad,
        gain_grad.reshape(16),
    )


def solution(mesh):
    fine = Mesh(mesh.devices.reshape(4, 2, 2, 4, 2), ("x", "zh", "c", "y", "zl"))
    dp, ctx = ("x", "zh", "c"), ("y", "zl")
    rows = P(dp, None, ctx, None, None)
    return jax.shard_map(
        body,
        mesh=fine,
        in_specs=(rows, P(), P(), P(dp, None), rows),
        out_specs=(rows, rows, P(dp + ctx, None), P(dp + ctx)),
        check_vma=False,
    )
```
